256 devices in a mesh: ctx: 32 (over y, z), head: 8 (over x, core).
Axes of the slice: x: 4, y: 4, z: 8, core: 2. Of those that a mesh axis runs over, the one named last changes fastest.
Arguments:
- qkv_tiles: bfloat16 [12288, 3, 3072], P('ctx', None, 'head'), may hold values from -100 to 100
- seq_pos: int32 [12288], P('ctx'), may hold values from 0 to 12287, as said below
- rope_pos: int32 [3, 12288], P(None, 'ctx'), may hold values from 0 to 79
- text_keys: bfloat16 [256, 3072], P('ctx', 'head'), may hold values from -100 to 100
- text_values: bfloat16 [256, 3072], P('ctx', 'head'), may hold values from -48 to 48
- text_len: int32 [1], replicated, may hold values from 32 to 256
- q_gain: float32 [128], replicated, may hold values from 0.8 to 1.7
- k_gain: float32 [128], replicated, may hold values from 0.8 to 1.7
- w_out: bfloat16 [3072, 3072], P('head'), may hold values from -0.75 to 0.75
- b_out: float32 [3072], P('head'), may hold values from -3 to 3
Outputs:
- mixed: bfloat16 [12288, 3072], P('ctx', 'head')
The draws below stay inside these ranges and needn't reach their ends.
Inputs may be any that keep to these rules, and one draw needn't show every extreme that they name: `seq_pos`: a permutation of the sequence positions; every owner sends to every context shard between 6 and 24 rows, exactly 24 to some shard; the multiset of these counts is the same for every owner and every shard; the rows one owner sends to one shard take a contiguous run of that shard's positions.
All inputs are finite; a program needn't handle non-finite values.
Results may differ from the reference program's by a relative error of at most 0.019.
Values may be sent and summed in bfloat16 or wider, within the bound.
A program may use at most 64 MiB of HBM per device.

```python
import math
import jax
import jax.numpy as jnp
from jax import lax

D = 3072
HEADS = 24
HD = 128
TOK_DEV = 384
TXT = 256
WINDOW = 3
TOKENS = 12288
N_CTX = 32
N_HEAD = 8


def route_positions(key):
    unit_rows = TOK_DEV // (2 * N_CTX)
    pattern = jnp.array([4, 2, 1, 1], jnp.int32)
    key_sizes, key_offsets, key_shuffle = jax.random.split(key, 3)
    piece_sizes = jax.random.permutation(key_sizes, jnp.tile(pattern, N_CTX // 4)) * unit_rows
    offsets = jax.random.permutation(key_offsets, jnp.arange(N_CTX, dtype=jnp.int32))
    piece_ends = jnp.cumsum(piece_sizes)
    row_ids = jnp.arange(TOK_DEV, dtype=jnp.int32)
    piece_index = jnp.sum((row_ids[:, None] >= piece_ends[None, :]).astype(jnp.int32), axis=1)
    owners = jnp.arange(N_CTX, dtype=jnp.int32)
    shard_of = (owners[:, None] - offsets[piece_index][None, :]) % N_CTX
    positions = shard_of * TOK_DEV + row_ids[None, :]
    owner_keys = jax.random.split(key_shuffle, N_CTX)

    def shuffle_one(one_key):
        return jax.random.permutation(one_key, TOK_DEV)
    shuffles = jax.vmap(shuffle_one)(owner_keys)
    positions = jnp.take_along_axis(positions, shuffles, axis=1)
    return positions.reshape(-1).astype(jnp.int32)


def channel_offsets(key):
    base = jax.random.fold_in(key, 11)
    return 1.5 * jnp.clip(jax.random.normal(base, (HEADS * HD,), jnp.float32), -4.0, 4.0)


def draw_seq_pos(key, part):
    return route_positions(key)


def draw_qkv_tiles(key, part):
    relative = route_positions(key).astype(jnp.float32) / TOKENS
    channel_bias = channel_offsets(key)
    key = jax.random.fold_in(key, 7)
    key_noise = jax.random.fold_in(key, 0)
    full_width = HEADS * HD
    noise_part = jnp.clip(jax.random.normal(key_noise, (TOKENS, 3, full_width), jnp.float32), -6.0, 6.0)
    rise_factor = 1.0 + 2.0 * relative
    component = jnp.array([1.0, 1.0, 4.0], jnp.float32)[None, :, None]
    shifted = jnp.array([0.0, 1.0, 0.0], jnp.float32)[None, :, None]
    offset_part = shifted * channel_bias[None, None, :] * rise_factor[:, None, None]
    return (noise_part * component + offset_part).astype(jnp.bfloat16)


def draw_text_keys(key, part):
    channel_bias = channel_offsets(key)
    key = jax.random.fold_in(key, 5)
    key_noise = jax.random.fold_in(key, 0)
    full_width = HEADS * HD
    noise_part = jnp.clip(jax.random.normal(key_noise, (TXT, full_width), jnp.float32), -6.0, 6.0)
    rise_level = 2.0
    return (noise_part + rise_level * channel_bias[None, :]).astype(jnp.bfloat16)


def place_ends(drawn, rng, smallest, high):
    place = [jax.random.randint(jax.random.fold_in(rng, axis), (), 0, length) for axis, length in enumerate(drawn.shape)]
    longest = drawn.shape.index(max(drawn.shape))
    next_to = place[:longest] + [(place[longest] + 1) % drawn.shape[longest]] + place[longest + 1:]
    return drawn.at[tuple(place)].set(smallest).at[tuple(next_to)].set(high)


def steps_of(stream_key, extent, shards, least, high):
    def one(axis_at, shards_of):
        steps = jax.random.uniform(jax.random.fold_in(jax.random.fold_in(stream_key, 6), axis_at), (shards_of,), jnp.float32, least / len(shards), high / len(shards))
        return jnp.repeat(jnp.exp(steps), extent[axis_at] // shards_of).reshape((-1,) + (1,) * (len(extent) - axis_at - 1))

    factor_of = one(*shards[0])
    for cut in shards[1:]:
        factor_of = factor_of * one(*cut)
    return factor_of


def scatter_about(rng, dims, deviation, limit, cuts=(), kind=jnp.bfloat16):
    drawn = deviation * jax.random.normal(rng, dims, jnp.float32)
    if cuts:
        drawn = drawn * steps_of(rng, dims, cuts, -0.22, 0.18)
    return jnp.clip(drawn, -limit, limit).astype(kind)


def setup_inputs(seed: int = 0) -> dict:
    keys = jax.random.split(jax.random.key(seed), 11)
    qkv_tiles = draw_qkv_tiles(jax.random.fold_in(keys[10], 71), 0)
    seq_pos = draw_seq_pos(jax.random.fold_in(keys[10], 71), 0)
    rope_pos = place_ends(jax.random.randint(keys[2], (3, TOKENS), 0, 80), jax.random.fold_in(keys[2], 1), 0, 79).astype(jnp.int32)
    text_keys = draw_text_keys(jax.random.fold_in(keys[10], 71), 0)
    text_values = scatter_about(keys[4], (TXT, HEADS * HD), 8.0, 48.0, ((0, 32), (1, 8)))
    text_len = jax.random.randint(keys[5], (1,), TXT // 8, TXT + 1).astype(jnp.int32)
    q_gain = jnp.clip(jnp.exp(jax.random.uniform(keys[6], (HD,), jnp.float32, math.log(0.8), math.log(1.7))), 0.8, 1.7)
    k_gain = jnp.clip(jnp.exp(jax.random.uniform(keys[7], (HD,), jnp.float32, math.log(0.8), math.log(1.7))), 0.8, 1.7)
    w_out = scatter_about(keys[8], (HEADS * HD, D), 64 ** -0.5, 0.75, ((0, 8),))
    b_out = scatter_about(keys[9], (D,), 0.5, 3.0, ((0, 8),), jnp.float32)
    return {"qkv_tiles": qkv_tiles, "seq_pos": seq_pos, "rope_pos": rope_pos, "text_keys": text_keys, "text_values": text_values, "text_len": text_len, "q_gain": q_gain, "k_gain": k_gain, "w_out": w_out, "b_out": b_out}


def rms_scale(x, gain_vec):
    return x * lax.rsqrt(lax.optimization_barrier(jnp.mean(x * x, axis=-1, keepdims=True)) + 1e-06) * gain_vec

def rope_tables(positions, head_dim):
    seg_time = head_dim // 8
    seg_space = (head_dim - seg_time) // 2
    tables = []
    for axis_index, seg_width in ((0, seg_time), (1, seg_space), (2, seg_space)):
        frequency = 256.0 ** (-jnp.arange(0, seg_width, 2, dtype=jnp.float32) / seg_width)
        angles = positions[axis_index].astype(jnp.float32)[:, None] * frequency[None, :]
        tables.append((jnp.cos(angles), jnp.sin(angles), seg_width))
    return tables

def rotate(x, tables):
    pieces = []
    offset = 0
    for cos_part, sin_part, seg_width in tables:
        half_width = seg_width // 2
        lower_part = x[..., offset:offset + half_width]
        upper_part = x[..., offset + half_width:offset + seg_width]
        cos_b = cos_part[:, None, :]
        sin_b = sin_part[:, None, :]
        pieces.append(lower_part * cos_b - upper_part * sin_b)
        pieces.append(upper_part * cos_b + lower_part * sin_b)
        offset += seg_width
    return jnp.concatenate(pieces, axis=-1)

def reference(qkv_tiles, seq_pos, rope_pos, text_keys, text_values, text_len, q_gain, k_gain, w_out, b_out):
    routed = jnp.zeros_like(qkv_tiles).at[seq_pos].set(qkv_tiles)
    shaped = routed.astype(jnp.float32).reshape(TOKENS, 3, HEADS, HD)
    query_n = rms_scale(shaped[:, 0], q_gain)
    key_n = rms_scale(shaped[:, 1], k_gain)
    key_mean = lax.optimization_barrier(jnp.sum(key_n, axis=0)) / TOKENS
    tables = rope_tables(rope_pos, HD)
    query_b = rotate(query_n, tables).astype(jnp.bfloat16)
    key_b = rotate(key_n - key_mean, tables).astype(jnp.bfloat16)
    value_b = routed[:, 2].reshape(TOKENS, HEADS, HD)
    text_kb = (rms_scale(text_keys.astype(jnp.float32).reshape(TXT, HEADS, HD), k_gain) - key_mean).astype(jnp.bfloat16)
    text_vb = text_values.reshape(TXT, HEADS, HD)
    text_live = jnp.arange(TXT, dtype=jnp.int32) < text_len[0]
    lead_rows = WINDOW * TOK_DEV
    key_pad = jnp.concatenate([jnp.zeros((lead_rows, HEADS, HD), jnp.bfloat16), key_b], axis=0)
    value_pad = jnp.concatenate([jnp.zeros((lead_rows, HEADS, HD), jnp.bfloat16), value_b], axis=0)

    def one_shard(shard_index):
        first_row = (shard_index * TOK_DEV).astype(jnp.int32)
        queries = lax.dynamic_slice_in_dim(query_b, first_row, TOK_DEV, 0)
        key_rows = lax.dynamic_slice_in_dim(key_pad, first_row, lead_rows + TOK_DEV, 0)
        value_rows = lax.dynamic_slice_in_dim(value_pad, first_row, lead_rows + TOK_DEV, 0)
        key_index = first_row - lead_rows + jnp.arange(lead_rows + TOK_DEV, dtype=jnp.int32)
        live_mask = jnp.concatenate([key_index >= 0, text_live])
        key_rows = jnp.concatenate([key_rows, text_kb], axis=0)
        value_rows = jnp.concatenate([value_rows, text_vb], axis=0)
        scores = jnp.einsum('qhd,khd->hqk', queries.astype(jnp.float32), key_rows.astype(jnp.float32)) * HD ** (-0.5)
        weights = jnp.where(live_mask[None, None, :], jnp.exp(scores), 0.0)
        running_sum = lax.optimization_barrier(jnp.sum(weights, axis=-1))
        rounded = lax.optimization_barrier(weights.astype(jnp.bfloat16)).astype(jnp.float32)
        numerator = jnp.einsum('hqk,khd->qhd', rounded, value_rows.astype(jnp.float32))
        return (numerator / running_sum.T[:, :, None]).astype(jnp.bfloat16)
    attended = lax.map(one_shard, jnp.arange(N_CTX, dtype=jnp.int32)).reshape(TOKENS, HEADS * HD)
    group_width = HEADS * HD // N_HEAD

    def one_group(running_sum, group_index):
        first_col = (group_index * group_width).astype(jnp.int32)
        attn_cols = lax.dynamic_slice_in_dim(attended, first_col, group_width, 1)
        weight_rows = lax.dynamic_slice_in_dim(w_out, first_col, group_width, 0)
        partial_out = jnp.dot(attn_cols, weight_rows, preferred_element_type=jnp.float32).astype(jnp.bfloat16)
        return (running_sum + lax.optimization_barrier(partial_out).astype(jnp.float32), None)
    running_sum, unused = lax.scan(one_group, jnp.zeros((TOKENS, D), jnp.float32), jnp.arange(N_HEAD, dtype=jnp.int32))
    return (running_sum + b_out[None, :]).astype(jnp.bfloat16)
```

```python
import functools

import jax
import jax.numpy as jnp
import numpy as np
from jax import lax
from jax.experimental import pallas as pl
from jax.experimental.pallas import tpu as pltpu
from jax.sharding import PartitionSpec as P

MESH = pl.DeviceIdType.MESH
BF = jnp.bfloat16
F32 = jnp.float32
NC = 32
NY, NZ = 4, 8
NH = 8
T = 384
HL = 3
HD = 128
CAP = 24
CUT = 16
ROWS = 9 * 16 + 5 * 16
WINDOW = 3
TXT = 256
TXD = 8
SCALE = float(np.log2(np.e) / np.sqrt(HD))


def iota(shape, axis):
    return lax.broadcasted_iota(jnp.int32, shape, axis)


def onehot(mask):
    return jnp.where(mask, 1.0, 0.0).astype(BF)


def dot(a, b, ca=1, cb=0):
    return lax.dot_general(a, b, (((ca,), (cb,)), ((), ())), preferred_element_type=F32)


def partner_of(lane):
    up = (lane < 8) | ((lane >= 16) & (lane < 44)) | ((lane >= 72) & (lane < 100))
    half = jnp.where(lane < 16, 8, 28)
    return jnp.where(up, lane + half, lane - half), up


def partner_rows(v):
    lane = iota(v.shape, 1)
    _, up = partner_of(lane)
    near = jnp.where(up, pltpu.roll(v, HD - 8, 1), pltpu.roll(v, 8, 1))
    far = jnp.where(up, pltpu.roll(v, HD - 28, 1), pltpu.roll(v, 28, 1))
    return jnp.where(lane < 16, near, far)


def rms_factor(x):
    return lax.rsqrt(jnp.mean(x * x, axis=-1, keepdims=True) + 1e-06)


def greet(peers):
    barrier = pltpu.get_barrier_semaphore()
    for peer in peers:
        pl.semaphore_signal(barrier, inc=1, device_id=peer, device_id_type=MESH)


def met(count):
    pl.semaphore_wait(pltpu.get_barrier_semaphore(), count)


def route_kernel(
    x_ref, pos_ref, rope_ref, tk_ref, tv_ref, qg_ref, kg_ref, freq_ref, w_ref,
    q_out, kv_out, t_out, wf_out,
    send, recv, tbuf, tab, ssem, rsem, tzs, tzr, tys, tyr, wss, wrs, lsem,
):
    me = lax.axis_index("ctx")
    hd = lax.axis_index("head")
    my, mz = me // NZ, me % NZ

    def signal_ctx(d, c):
        pl.semaphore_signal(
            pltpu.get_barrier_semaphore(), inc=1,
            device_id=((me + d) % NC, hd), device_id_type=MESH,
        )
        return c

    lax.fori_loop(1, NC, signal_ctx, 0)
    greet([(me, (hd + d) % NH) for d in range(1, NH)])

    pos = pos_ref[...]
    shard = ((pos >> 7) * 171) >> 9
    mine = iota((NC, T), 0) == shard
    first = jnp.min(jnp.where(mine, pos, 1 << 20), axis=1, keepdims=True)
    count = jnp.sum(jnp.where(mine, 1, 0), axis=1, keepdims=True)
    rank = pos - jnp.sum(jnp.where(mine, first, 0), axis=0, keepdims=True)
    code_a = jnp.where(rank < CUT, shard * 16 + rank, -100)
    code_b = jnp.where(rank < CUT, -100, shard * 16 + rank - CUT)
    slot = iota((NC * 16, T), 0)
    pick_a = onehot(slot == code_a)
    pick_b = onehot((slot == code_b) | (slot == code_b + 8))

    kg = kg_ref[...]
    sub16 = iota((16, HD), 0)
    extra = jnp.zeros((16, HD), F32)
    for h in range(HL):
        k = x_ref[1, :, h * HD:(h + 1) * HD].astype(F32)
        total = jnp.sum(k * rms_factor(k), axis=0, keepdims=True) * kg
        high = total.astype(BF).astype(F32)
        extra = jnp.where(sub16 == 9 + h, high, extra)
        extra = jnp.where(sub16 == 12 + h, total - high, extra)
    start = first - iota((NC, 1), 0) * T
    lane = iota((NC, HD), 1)
    meta = jnp.where(lane < 32, start >> 4, jnp.where(lane < 64, start & 15, count)).astype(F32)
    row3 = iota((NC, 16, HD), 1)
    extra = jnp.where(row3 == 8, meta[:, None, :], extra[None])

    for c in range(9):
        block = x_ref[c // 3, :, (c % 3) * HD:(c % 3 + 1) * HD]
        send[:, c * 16:(c + 1) * 16, :] = dot(pick_a, block).astype(BF).reshape(NC, 16, HD)
        late = dot(pick_b, block).reshape(NC, 16, HD)
        if c % 2 == 0:
            even = late
        else:
            base = 144 + (c // 2) * 16
            send[:, base:base + 16, :] = jnp.where(row3 < 8, even, late).astype(BF)
    send[:, 208:224, :] = jnp.where(row3 < 8, even, extra).astype(BF)
    tbuf[my, mz] = jnp.concatenate(
        [tk_ref[...].astype(F32), tv_ref[...].astype(F32)], axis=0
    ).astype(BF)
    recv[me] = send[me]

    met(NC - 1 + NH - 1)

    def text_z(d):
        z = (mz + d) % NZ
        return pltpu.make_async_remote_copy(
            src_ref=tbuf.at[my, mz], dst_ref=tbuf.at[my, mz], send_sem=tzs.at[d], recv_sem=tzr.at[d],
            device_id=(my * NZ + z, hd), device_id_type=MESH,
        )

    def text_y(d):
        y = (my + d) % NY
        return pltpu.make_async_remote_copy(
            src_ref=tbuf.at[my], dst_ref=tbuf.at[my], send_sem=tys.at[d], recv_sem=tyr.at[d],
            device_id=(y * NZ + mz, hd), device_id_type=MESH,
        )

    def piece(d):
        to = (me + d) % NC
        return pltpu.make_async_remote_copy(
            src_ref=send.at[to], dst_ref=recv.at[me], send_sem=ssem.at[d], recv_sem=rsem.at[d],
            device_id=(to, hd), device_id_type=MESH,
        )

    def weight(d):
        to = (hd + d) % NH
        return pltpu.make_async_remote_copy(
            src_ref=w_ref.at[:, :, pl.ds(pl.multiple_of(to * T, T), T)],
            dst_ref=wf_out.at[:, pl.ds(pl.multiple_of(hd * HD, HD), HD), :],
            send_sem=wss.at[d], recv_sem=wrs.at[d],
            device_id=(me, to), device_id_type=MESH,
        )

    def start_of(make):
        def go(d, c):
            make(d).start()
            return c
        return go

    def landed(make):
        def go(d, c):
            make(d).wait_recv()
            return c
        return go

    def left(make):
        def go(d, c):
            make(d).wait_send()
            return c
        return go

    lax.fori_loop(1, NZ, start_of(text_z), 0)
    lax.fori_loop(1, NC, start_of(piece), 0)
    lax.fori_loop(1, NH, start_of(weight), 0)
    own_w = pltpu.make_async_copy(
        w_ref.at[:, :, pl.ds(pl.multiple_of(hd * T, T), T)],
        wf_out.at[:, pl.ds(pl.multiple_of(hd * HD, HD), HD), :], lsem,
    )
    own_w.start()

    lane_t = iota((T, HD), 1)
    _, up = partner_of(lane_t)
    eye = iota((T, T), 0) == iota((T, T), 1)
    col = []
    for a in range(3):
        row = rope_ref[a:a + 1, :].astype(F32)
        col.append(jnp.sum(jnp.where(eye, row, 0.0), axis=1, keepdims=True))
    at = jnp.where(lane_t < 16, col[0], jnp.where(lane_t < 72, col[1], col[2]))
    angle = at * freq_ref[...]
    tab[0] = jnp.cos(angle)
    sine = jnp.sin(angle)
    tab[1] = jnp.where(up, -sine, sine)

    lax.fori_loop(1, NZ, landed(text_z), 0)
    lax.fori_loop(1, NY, start_of(text_y), 0)
    lax.fori_loop(1, NC, landed(piece), 0)

    tail = recv[:, 208:224, :].astype(F32)
    sums = jnp.sum(tail, axis=0)
    info = tail[:, 8, :]
    begin = info[:, 0:1] * 16.0 + info[:, 32:33]
    size = info[:, 64:65]
    lane_s = iota((NC, NC * 16), 1)
    owner = (lane_s >> 4) == iota((NC, NC * 16), 0)
    begin_r = jnp.sum(jnp.where(owner, begin, 0.0), axis=0, keepdims=True)
    size_r = jnp.sum(jnp.where(owner, size, 0.0), axis=0, keepdims=True)
    off = iota((1, NC * 16), 1) & 15
    offf = off.astype(F32)
    dest_a = jnp.where(offf < size_r, begin_r + offf, -1.0)
    off_l = offf + 16.0
    dest_l = jnp.where((off < 8) & (off_l < size_r), begin_r + off_l, -1.0)
    off_h = offf + 8.0
    dest_h = jnp.where((off >= 8) & (off_h < size_r), begin_r + off_h, -1.0)
    place = iota((T, NC * 16), 0).astype(F32)
    put_a = onehot(place == dest_a)
    put_l = onehot(place == dest_l)
    put_h = onehot(place == dest_h)

    def routed(c):
        base = 144 + (c // 2) * 16
        return dot(put_a, recv[:, c * 16:(c + 1) * 16, :].reshape(NC * 16, HD)) + dot(
            put_l if c % 2 == 0 else put_h, recv[:, base:base + 16, :].reshape(NC * 16, HD)
        )

    li, lj = iota((HD, HD), 0), iota((HD, HD), 1)
    swap = onehot(li == partner_of(lj)[0])
    qg = qg_ref[...]
    cos, sin = tab[0], tab[1]

    def rotated(x, gain):
        pair = dot(x.astype(BF), swap)
        gain_p = partner_rows(jnp.broadcast_to(gain, (8, HD)))[0:1]
        return rms_factor(x) * (x * (cos * gain) + pair * (sin * gain_p))

    means = []
    for h in range(HL):
        mean = (sums[9 + h:10 + h] + sums[12 + h:13 + h]) * (1.0 / (NC * T))
        means.append(mean)
        mean_p = partner_rows(jnp.broadcast_to(mean, (8, HD)))[0:1]
        k = rotated(routed(3 + h), kg) - (cos * mean + sin * mean_p)
        kv_out[h, 0] = k.astype(BF)
        kv_out[h, 1] = routed(6 + h).astype(BF)
        q_out[h] = rotated(routed(h), qg).astype(BF)

    lax.fori_loop(1, NY, landed(text_y), 0)
    for h in range(HL):
        block = tbuf[:, :, :, h * HD:(h + 1) * HD].astype(F32).reshape(NC, 16, HD)
        k = block[:, :TXD].reshape(TXT, HD)
        t_out[0, h] = (k * rms_factor(k) * kg - means[h]).astype(BF)
        t_out[1, h] = block[:, TXD:].reshape(TXT, HD).astype(BF)

    own_w.wait()
    lax.fori_loop(1, NZ, left(text_z), 0)
    lax.fori_loop(1, NY, left(text_y), 0)
    lax.fori_loop(1, NC, left(piece), 0)
    lax.fori_loop(1, NH, left(weight), 0)
    lax.fori_loop(1, NH, landed(weight), 0)


def attend_kernel(
    q_ref, kv_ref, t_ref, len_ref, wf_ref, b_ref, o_ref,
    win, att, wv, ws, wr, xs, xr, fs, fr, lsem,
):
    me = lax.axis_index("ctx")
    hd = lax.axis_index("head")
    ahead, behind = (me + 1) % NC, (me + NC - 1) % NC
    core = hd % 2
    sib = hd + 1 - 2 * core
    greet([(ahead, hd), (behind, hd), (me, sib)] + [(me, (hd + 2 * e) % NH) for e in (1, 2, 3)])
    load_w = pltpu.make_async_copy(wf_ref, wv, lsem)
    load_w.start()
    met(6)

    def shift(d, h):
        return pltpu.make_async_remote_copy(
            src_ref=kv_ref.at[h] if d == 0 else win.at[d - 1, h], dst_ref=win.at[d, h],
            send_sem=ws.at[d, h], recv_sem=wr.at[d, h],
            device_id=(ahead, hd), device_id_type=MESH,
        )

    def spread(h, e):
        return pltpu.make_async_remote_copy(
            src_ref=att.at[h, hd], dst_ref=att.at[h, hd],
            send_sem=xs.at[h, e], recv_sem=xr.at[h, e],
            device_id=(me, (hd + 2 * e) % NH if e else sib), device_id_type=MESH,
        )

    def hand_on(h, e):
        g = (hd + NH - 2 * e) % NH
        return pltpu.make_async_remote_copy(
            src_ref=att.at[h, g], dst_ref=att.at[h, g],
            send_sem=fs.at[h, e], recv_sem=fr.at[h, e],
            device_id=(me, sib), device_id_type=MESH,
        )

    ones = jnp.ones((T, HD), BF)
    live = iota((TXT, 2 * HD), 0) < len_ref[0]

    def weigh(h, k, v_ext):
        p = jnp.exp2(dot(q_ref[h], k, 1, 1) * SCALE)
        return dot(p.astype(BF), v_ext)

    shift(0, 0).start()
    shift(0, 1).start()

    acc = {}
    for h in range(HL):
        own = weigh(h, kv_ref[h, 0], jnp.concatenate([kv_ref[h, 1], ones], axis=1))
        tv = jnp.concatenate([t_ref[1, h], ones[:TXT]], axis=1)
        tv = jnp.where(live, tv.astype(F32), 0.0).astype(BF)
        acc[h] = own + weigh(h, t_ref[0, h], tv)

    def arrive(d, h):
        shift(d, h).wait_recv()
        if d < WINDOW - 1:
            shift(d + 1, h).start()
        part = weigh(h, win[d, h, 0], jnp.concatenate([win[d, h, 1], ones], axis=1))
        acc[h] = acc[h] + jnp.where(me > d, part, 0.0)

    def finish(h):
        att[h, hd] = (acc[h][:, :HD] / acc[h][:, HD:]).astype(BF)
        for e in (2, 1, 3, 0):
            spread(h, e).start()

    arrive(0, 0)
    arrive(0, 1)
    shift(0, 2).start()
    arrive(1, 0)
    arrive(1, 1)
    arrive(0, 2)
    arrive(2, 0)
    finish(0)
    arrive(2, 1)
    finish(1)
    arrive(1, 2)
    arrive(2, 2)
    finish(2)
    load_w.wait()
    out = jnp.zeros((T, T), F32)
    for h in range(HL):
        for e in (1, 3, 2):
            spread(h, e).wait_recv()
            hand_on(h, e).start()
        spread(h, 0).wait_recv()
        for e in (1, 3, 2):
            hand_on(h, e).wait_recv()
        left = jnp.concatenate([att[h, g] for g in range(NH)], axis=1)
        out = out + dot(left, wv[h])
    o_ref[...] = (out + b_ref[...]).astype(BF)

    for d in range(WINDOW):
        for h in range(HL):
            shift(d, h).wait_send()
    for h in range(HL):
        for e in range(4):
            spread(h, e).wait_send()
        for e in range(1, 4):
            hand_on(h, e).wait_send()


def freq_row():
    row = np.zeros((1, HD), np.float32)
    offset = 0
    for width in (16, 56, 56):
        f = np.float32(256.0) ** (-np.arange(0, width, 2, dtype=np.float32) / np.float32(width))
        row[0, offset:offset + width] = np.concatenate([f, f])
        offset += width
    return row


def on_device(
    qkv_tiles, seq_pos, rope_pos, text_keys, text_values, text_len, q_gain, k_gain, w_out, b_out
):
    vmem = pl.BlockSpec(memory_space=pltpu.VMEM)
    hbm = pl.BlockSpec(memory_space=pl.ANY)
    smem = pl.BlockSpec(memory_space=pltpu.SMEM)
    dma = pltpu.SemaphoreType.DMA
    q, kv, t, wf = pl.pallas_call(
        route_kernel,
        out_shape=(
            jax.ShapeDtypeStruct((HL, T, HD), BF),
            jax.ShapeDtypeStruct((HL, 2, T, HD), BF),
            jax.ShapeDtypeStruct((2, HL, TXT, HD), BF),
            jax.ShapeDtypeStruct((HL, NH * HD, T), BF),
        ),
        in_specs=[vmem] * 8 + [hbm],
        out_specs=(vmem, vmem, vmem, hbm),
        scratch_shapes=[
            pltpu.VMEM((NC, ROWS, HD), BF),
            pltpu.VMEM((NC, ROWS, HD), BF),
            pltpu.VMEM((NY, NZ, 16, T), BF),
            pltpu.VMEM((2, T, HD), F32),
            dma((NC,)), dma((NC,)), dma((NZ,)), dma((NZ,)), dma((NY,)), dma((NY,)),
            dma((NH,)), dma((NH,)), dma,
        ],
        compiler_params=pltpu.CompilerParams(
            collective_id=0, has_side_effects=True, vmem_limit_bytes=48 << 20
        ),
        name="route",
    )(
        qkv_tiles.transpose(1, 0, 2),
        seq_pos.reshape(1, T),
        rope_pos,
        text_keys,
        text_values,
        q_gain.reshape(1, HD),
        k_gain.reshape(1, HD),
        jnp.asarray(freq_row()),
        w_out.reshape(HL, HD, NH * T),
    )
    return pl.pallas_call(
        attend_kernel,
        out_shape=jax.ShapeDtypeStruct((T, T), BF),
        in_specs=[vmem, vmem, vmem, smem, hbm, vmem],
        out_specs=vmem,
        scratch_shapes=[
            pltpu.VMEM((WINDOW, HL, 2, T, HD), BF),
            pltpu.VMEM((HL, NH, T, HD), BF),
            pltpu.VMEM((HL, NH * HD, T), BF),
            dma((WINDOW, HL)), dma((WINDOW, HL)), dma((HL, 4)), dma((HL, 4)),
            dma((HL, 4)), dma((HL, 4)), dma,
        ],
        compiler_params=pltpu.CompilerParams(
            collective_id=1, has_side_effects=True, vmem_limit_bytes=48 << 20
        ),
        name="attend",
    )(q, kv, t, text_len, wf, b_out.reshape(1, T))


def solution(mesh):
    in_specs = (
        P("ctx", None, "head"),
        P("ctx"),
        P(None, "ctx"),
        P("ctx", "head"),
        P("ctx", "head"),
        P(),
        P(),
        P(),
        P("head", None),
        P("head"),
    )
    return jax.shard_map(
        on_device, mesh=mesh, in_specs=in_specs, out_specs=P("ctx", "head"), check_vma=False
    )
```

```python
import functools

import jax
import jax.numpy as jnp
import numpy as np
from jax import lax
from jax.experimental import pallas as pl
from jax.experimental.pallas import tpu as pltpu
from jax.sharding import PartitionSpec as P

MESH = pl.DeviceIdType.MESH
BF = jnp.bfloat16
F32 = jnp.float32
NC = 32
NY, NZ = 4, 8
NH = 8
T = 384
HL = 3
HD = 128
CUT = 16
KV_ROWS = 160
ROWS = 224
WINDOW = 3
TXT = 256
TXD = 8
GROUP = 8
SCALE = float(np.log2(np.e) / np.sqrt(HD))

OFFSETS = sorted(
    ((dy, dz) for dy in range(NY) for dz in range(NZ) if dy or dz),
    key=lambda o: -(2 * min(o[1], NZ - o[1]) + min(o[0], NY - o[0])),
)


def iota(shape, axis):
    return lax.broadcasted_iota(jnp.int32, shape, axis)


def onehot(mask):
    return jnp.where(mask, 1.0, 0.0).astype(BF)


def dot(a, b, ca=1, cb=0):
    return lax.dot_general(a, b, (((ca,), (cb,)), ((), ())), preferred_element_type=F32)


def partner_of(lane):
    up = (lane < 8) | ((lane >= 16) & (lane < 44)) | ((lane >= 72) & (lane < 100))
    half = jnp.where(lane < 16, 8, 28)
    return jnp.where(up, lane + half, lane - half), up


def partner_row(v):
    v = jnp.broadcast_to(v, (8, HD))
    lane = iota(v.shape, 1)
    _, up = partner_of(lane)
    near = jnp.where(up, pltpu.roll(v, HD - 8, 1), pltpu.roll(v, 8, 1))
    far = jnp.where(up, pltpu.roll(v, HD - 28, 1), pltpu.roll(v, 28, 1))
    return jnp.where(lane < 16, near, far)[0:1]


def rms_factor(x):
    return lax.rsqrt(jnp.mean(x * x, axis=-1, keepdims=True) + 1e-06)


def kernel(
    x_hbm, pos_hbm, rope_hbm, tk_hbm, tv_hbm, len_ref, qg_hbm, kg_hbm, freq_hbm, w_hbm, b_hbm,
    o_ref,
    x, pos_v, rope, rope_far, tk, tv, qg_v, kg_v, freq, bias,
    send, recv, tbuf, tab, puts, acc, qb, kv, text, win, stage, att, wv,
    isem, ssem, rsem, tzs, tzr, tys, tyr, wss, wrs, rs, rr,
    ws, wr, hs, hr, xs, xr, fs, fr,
):
    me = lax.axis_index("ctx")
    hd = lax.axis_index("head")
    my, mz = me // NZ, me % NZ
    core = hd % 2
    sib = hd + 1 - 2 * core

    def home(s):
        z = s % NZ
        return s - z + z + core * (NZ - 1 - 2 * z)

    mirror = my * NZ + NZ - 1 - mz
    shard_me = home(me)
    ahead = home((shard_me + 1) % NC)

    def at(offset):
        return ((my + offset[0]) % NY) * NZ + (mz + offset[1]) % NZ

    barrier = pltpu.get_barrier_semaphore()

    def greet_ctx(d, c):
        pl.semaphore_signal(barrier, inc=1, device_id=((me + d) % NC, hd), device_id_type=MESH)
        return c

    def greet_head(d, c):
        pl.semaphore_signal(barrier, inc=1, device_id=(me, (hd + d) % NH), device_id_type=MESH)
        return c

    fetch = [
        pltpu.make_async_copy(src, dst, isem.at[i])
        for i, (src, dst) in enumerate([
            (pos_hbm, pos_v), (x_hbm.at[1], x.at[1]), (kg_hbm, kg_v), (x_hbm.at[2], x.at[2]),
            (tk_hbm, tk), (tv_hbm, tv), (rope_hbm, rope), (x_hbm.at[0], x.at[0]),
            (freq_hbm, freq), (qg_hbm, qg_v), (b_hbm, bias),
            (
                w_hbm.at[:, :, pl.ds(pl.multiple_of(hd * T, T), T)],
                wv.at[:, pl.ds(pl.multiple_of(hd * HD, HD), HD), :],
            ),
        ])
    ]
    for copy in fetch:
        copy.start()
    lax.fori_loop(1, NC, greet_ctx, 0)
    lax.fori_loop(1, NH, greet_head, 0)

    fetch[0].wait()
    pos = pos_v[...]
    shard = ((pos >> 7) * 171) >> 9
    mine = iota((NC, T), 0) == shard
    first = jnp.min(jnp.where(mine, pos, 1 << 20), axis=1, keepdims=True)
    count = jnp.sum(jnp.where(mine, 1, 0), axis=1, keepdims=True)
    rank = pos - jnp.sum(jnp.where(mine, first, 0), axis=0, keepdims=True)
    code_a = jnp.where(rank < CUT, shard * 16 + rank, -100)
    code_b = jnp.where(rank < CUT, -100, shard * 16 + rank - CUT)
    slot = iota((NC * 16, T), 0)
    pick_a = onehot(slot == code_a)
    pick_b = onehot((slot == code_b) | (slot == code_b + 8))

    fetch[1].wait()
    fetch[2].wait()
    kg = kg_v[...]
    sub16 = iota((16, HD), 0)
    extra = jnp.zeros((16, HD), F32)
    for h in range(HL):
        k = x[1, :, h * HD:(h + 1) * HD].astype(F32)
        total = jnp.sum(k * rms_factor(k), axis=0, keepdims=True) * kg
        high = total.astype(BF).astype(F32)
        extra = jnp.where(sub16 == 9 + h, high, extra)
        extra = jnp.where(sub16 == 12 + h, total - high, extra)
    start = first - iota((NC, 1), 0) * T
    lane = iota((NC, HD), 1)
    meta = jnp.where(lane < 32, start >> 4, jnp.where(lane < 64, start & 15, count)).astype(F32)
    row3 = iota((NC, 16, HD), 1)
    extra = jnp.where(row3 == 8, meta[:, None, :], extra[None])

    def early(comp, h):
        block = x[comp, :, h * HD:(h + 1) * HD]
        return dot(pick_a, block).astype(BF).reshape(NC, 16, HD)

    def late(comp, h):
        return dot(pick_b, x[comp, :, h * HD:(h + 1) * HD]).reshape(NC, 16, HD)

    def both(a, b):
        return jnp.where(row3 < 8, a, b).astype(BF)

    fetch[3].wait()
    fetch[7].wait()
    for c in range(6):
        send[:, c * 16:(c + 1) * 16, :] = early(1 + c // 3, c % 3)
    send[:, 96:112, :] = both(late(1, 0), late(1, 1))
    send[:, 112:128, :] = both(late(1, 2), late(2, 0))
    send[:, 128:144, :] = both(late(2, 1), late(2, 2))
    send[:, 144:160, :] = both(late(0, 2), extra)
    recv[NC - 1, 0:KV_ROWS] = send[shard_me, 0:KV_ROWS]
    fetch[4].wait()
    fetch[5].wait()
    tbuf[my, mz] = jnp.concatenate([tk[...].astype(F32), tv[...].astype(F32)], axis=0).astype(BF)
    fetch[6].wait()

    pl.semaphore_wait(barrier, NC - 1 + NH - 1)

    def text_z(d):
        z = (mz + d) % NZ
        return pltpu.make_async_remote_copy(
            src_ref=tbuf.at[my, mz], dst_ref=tbuf.at[my, mz], send_sem=tzs.at[d], recv_sem=tzr.at[d],
            device_id=(my * NZ + z, hd), device_id_type=MESH,
        )

    def text_y(d):
        y = (my + d) % NY
        return pltpu.make_async_remote_copy(
            src_ref=tbuf.at[my], dst_ref=tbuf.at[my], send_sem=tys.at[d], recv_sem=tyr.at[d],
            device_id=(y * NZ + mz, hd), device_id_type=MESH,
        )

    def piece(i, part):
        to = at(OFFSETS[i])
        rows = pl.ds(0, KV_ROWS) if part == 0 else pl.ds(KV_ROWS, ROWS - KV_ROWS)
        return pltpu.make_async_remote_copy(
            src_ref=send.at[home(to), rows], dst_ref=recv.at[i, rows],
            send_sem=ssem.at[part, i], recv_sem=rsem.at[part, i],
            device_id=(to, hd), device_id_type=MESH,
        )

    def weight(d):
        to = (hd + d) % NH
        return pltpu.make_async_remote_copy(
            src_ref=w_hbm.at[:, :, pl.ds(pl.multiple_of(to * T, T), T)],
            dst_ref=wv.at[:, pl.ds(pl.multiple_of(hd * HD, HD), HD), :],
            send_sem=wss.at[d], recv_sem=wrs.at[d],
            device_id=(me, to), device_id_type=MESH,
        )

    rope_swap = pltpu.make_async_remote_copy(
        src_ref=rope, dst_ref=rope_far, send_sem=rs, recv_sem=rr,
        device_id=(mirror, hd), device_id_type=MESH,
    )

    def shift(d, h):
        return pltpu.make_async_remote_copy(
            src_ref=kv.at[h] if d == 0 else win.at[d - 1, h], dst_ref=win.at[d, h],
            send_sem=ws.at[d, h], recv_sem=wr.at[d, h],
            device_id=(ahead, hd), device_id_type=MESH,
        )

    def go_home(h):
        return pltpu.make_async_remote_copy(
            src_ref=stage.at[h], dst_ref=att.at[h, hd], send_sem=hs.at[h], recv_sem=hr.at[h],
            device_id=(mirror, hd), device_id_type=MESH,
        )

    def spread(h, e):
        return pltpu.make_async_remote_copy(
            src_ref=att.at[h, hd], dst_ref=att.at[h, hd],
            send_sem=xs.at[h, e], recv_sem=xr.at[h, e],
            device_id=(me, (hd + 2 * e) % NH if e else sib), device_id_type=MESH,
        )

    def hand_on(h, e):
        g = (hd + NH - 2 * e) % NH
        return pltpu.make_async_remote_copy(
            src_ref=att.at[h, g], dst_ref=att.at[h, g],
            send_sem=fs.at[h, e], recv_sem=fr.at[h, e],
            device_id=(me, sib), device_id_type=MESH,
        )

    def each(make, n, act):
        def go(d, c):
            getattr(make(d), act)()
            return c
        lax.fori_loop(1, n, go, 0)

    rope_swap.start()
    each(text_z, NZ, "start")
    for i in range(NC - 1):
        piece(i, 0).start()

    for h in range(HL):
        send[:, 160 + h * 16:176 + h * 16, :] = early(0, h)
    send[:, 208:224, :] = both(late(0, 0), late(0, 1))
    recv[NC - 1, KV_ROWS:ROWS] = send[shard_me, KV_ROWS:ROWS]
    for i in range(NC - 1):
        piece(i, 1).start()
    each(weight, NH, "start")

    fetch[8].wait()
    fetch[9].wait()
    rope_swap.wait_recv()
    lane_t = iota((T, HD), 1)
    _, up = partner_of(lane_t)
    eye = iota((T, T), 0) == iota((T, T), 1)
    col = []
    for a in range(3):
        row = jnp.where(core == 1, rope_far[a:a + 1, :], rope[a:a + 1, :]).astype(F32)
        col.append(jnp.sum(jnp.where(eye, row, 0.0), axis=1, keepdims=True))
    angle = jnp.where(lane_t < 16, col[0], jnp.where(lane_t < 72, col[1], col[2])) * freq[...]
    tab[0] = jnp.cos(angle)
    sine = jnp.sin(angle)
    tab[1] = jnp.where(up, -sine, sine)
    li, lj = iota((HD, HD), 0), iota((HD, HD), 1)
    swap = onehot(li == partner_of(lj)[0])

    each(text_z, NZ, "wait_recv")
    each(text_y, NY, "start")

    W = GROUP * 16
    off = iota((1, W), 1) & 15
    offf = off.astype(F32)
    owner = (iota((GROUP, W), 1) >> 4) == iota((GROUP, W), 0)
    place = iota((T, W), 0).astype(F32)
    sums = jnp.zeros((16, HD), F32)

    def rows_of(g, base):
        return recv[g * GROUP:(g + 1) * GROUP, base:base + 16, :].reshape(W, HD)

    def put(g, first_base, last_base, high):
        return dot(puts[g, 0], rows_of(g, first_base)) + dot(
            puts[g, 2 if high else 1], rows_of(g, last_base)
        )

    for g in range(NC // GROUP):
        for i in range(g * GROUP, min((g + 1) * GROUP, NC - 1)):
            piece(i, 0).wait_recv()
        tail = recv[g * GROUP:(g + 1) * GROUP, 144:160, :].astype(F32)
        sums = sums + jnp.sum(tail, axis=0)
        info = tail[:, 8, :]
        begin = jnp.sum(
            jnp.where(owner, info[:, 0:1] * 16.0 + info[:, 32:33], 0.0), axis=0, keepdims=True
        )
        size = jnp.sum(jnp.where(owner, info[:, 64:65], 0.0), axis=0, keepdims=True)
        puts[g, 0] = onehot(place == jnp.where(offf < size, begin + offf, -1.0))
        low = (off < 8) & (offf + 16.0 < size)
        puts[g, 1] = onehot(place == jnp.where(low, begin + offf + 16.0, -1.0))
        high = (off >= 8) & (offf + 8.0 < size)
        puts[g, 2] = onehot(place == jnp.where(high, begin + offf + 8.0, -1.0))
        for c in range(6):
            part = put(g, c * 16, 96 + (c // 2) * 16, c % 2)
            acc[c] = part if g == 0 else acc[c] + part

    cos, sin = tab[0], tab[1]

    def rotated(rows, gain):
        pair = dot(rows.astype(BF), swap)
        return rms_factor(rows) * (rows * (cos * gain) + pair * (sin * partner_row(gain)))

    means = []
    for h in range(HL):
        mean = (sums[9 + h:10 + h] + sums[12 + h:13 + h]) * (1.0 / (NC * T))
        means.append(mean)
        k = rotated(acc[h], kg) - (cos * mean + sin * partner_row(mean))
        kv[h, 0] = k.astype(BF)
        kv[h, 1] = acc[3 + h].astype(BF)
        if h < 2:
            shift(0, h).start()

    each(text_y, NY, "wait_recv")
    for h in range(HL):
        block = tbuf[:, :, :, h * HD:(h + 1) * HD].astype(F32).reshape(NC, 16, HD)
        k = block[:, :TXD].reshape(TXT, HD)
        text[0, h] = (k * rms_factor(k) * kg - means[h]).astype(BF)
        v = jnp.where(iota((TXT, HD), 0) < len_ref[0], block[:, TXD:].reshape(TXT, HD), 0.0)
        text[1, h] = v.astype(BF)

    def forward(d, h):
        shift(d, h).wait_recv()
        if d < WINDOW - 1:
            shift(d + 1, h).start()

    forward(0, 0)
    forward(0, 1)
    shift(0, 2).start()

    qg = qg_v[...]
    for g in range(NC // GROUP):
        for i in range(g * GROUP, min((g + 1) * GROUP, NC - 1)):
            piece(i, 1).wait_recv()
    for h in range(HL):
        rows = None
        for g in range(NC // GROUP):
            part = put(g, 160 + h * 16, 208 if h < 2 else 144, h == 1)
            rows = part if rows is None else rows + part
        qb[h] = rotated(rows, qg).astype(BF)

    ones = jnp.ones((T, HD), BF)
    live = onehot(iota((TXT, HD), 0) < len_ref[0])

    def weigh(h, k, v, beside):
        p = jnp.exp2(dot(qb[h], k, 1, 1) * SCALE)
        return dot(p.astype(BF), jnp.concatenate([v, beside], axis=1))

    num = {}
    for h in range(HL):
        num[h] = weigh(h, kv[h, 0], kv[h, 1], ones) + weigh(h, text[0, h], text[1, h], live)

    def attend(d, h):
        part = weigh(h, win[d, h, 0], win[d, h, 1], ones)
        num[h] = num[h] + jnp.where(shard_me > d, part, 0.0)

    def arrive(d, h):
        forward(d, h)
        attend(d, h)

    def spread_all(h):
        for e in (2, 1, 3, 0):
            spread(h, e).start()

    def finish(h):
        done = (num[h][:, :HD] / num[h][:, HD:]).astype(BF)

        @pl.when(core == 0)
        def _():
            att[h, hd] = done
            spread_all(h)

        @pl.when(core == 1)
        def _():
            stage[h] = done
            go_home(h).start()

    def relay(h):
        @pl.when(core == 1)
        def _():
            go_home(h).wait_recv()
            spread_all(h)

    def hand(h):
        for e in (1, 3, 2):
            spread(h, e).wait_recv()
            hand_on(h, e).start()

    def project(h):
        spread(h, 0).wait_recv()
        for e in (1, 3, 2):
            hand_on(h, e).wait_recv()
        rows = jnp.concatenate([att[h, g] for g in range(NH)], axis=1)
        return dot(rows, wv[h])

    attend(0, 0)
    attend(0, 1)
    arrive(1, 0)
    arrive(1, 1)
    arrive(0, 2)
    arrive(2, 0)
    finish(0)
    arrive(2, 1)
    finish(1)
    relay(0)
    arrive(1, 2)
    arrive(2, 2)
    finish(2)
    relay(1)
    each(weight, NH, "wait_recv")
    fetch[10].wait()
    fetch[11].wait()
    hand(0)
    out = project(0) + bias[...]
    relay(2)
    hand(1)
    out = out + project(1)
    hand(2)
    out = out + project(2)
    o_ref[...] = out.astype(BF)

    rope_swap.wait_send()
    each(text_z, NZ, "wait_send")
    each(text_y, NY, "wait_send")
    each(weight, NH, "wait_send")
    for i in range(NC - 1):
        piece(i, 0).wait_send()
        piece(i, 1).wait_send()
    for h in range(HL):
        for d in range(WINDOW):
            shift(d, h).wait_send()
        for e in range(4):
            spread(h, e).wait_send()
        for e in range(1, 4):
            hand_on(h, e).wait_send()

    @pl.when(core == 1)
    def _():
        for h in range(HL):
            go_home(h).wait_send()


def freq_row():
    row = np.zeros((1, HD), np.float32)
    offset = 0
    for width in (16, 56, 56):
        f = np.float32(256.0) ** (-np.arange(0, width, 2, dtype=np.float32) / np.float32(width))
        row[0, offset:offset + width] = np.concatenate([f, f])
        offset += width
    return row


def on_device(
    qkv_tiles, seq_pos, rope_pos, text_keys, text_values, text_len, q_gain, k_gain, w_out, b_out
):
    hbm = pl.BlockSpec(memory_space=pl.ANY)
    smem = pl.BlockSpec(memory_space=pltpu.SMEM)
    vmem = pltpu.VMEM
    dma = pltpu.SemaphoreType.DMA
    return pl.pallas_call(
        kernel,
        out_shape=jax.ShapeDtypeStruct((T, T), BF),
        in_specs=[hbm] * 5 + [smem] + [hbm] * 5,
        out_specs=pl.BlockSpec(memory_space=pltpu.VMEM),
        scratch_shapes=[
            vmem((3, T, T), BF),
            vmem((1, T), jnp.int32),
            vmem((3, T), jnp.int32),
            vmem((3, T), jnp.int32),
            vmem((TXD, T), BF),
            vmem((TXD, T), BF),
            vmem((1, HD), F32),
            vmem((1, HD), F32),
            vmem((1, HD), F32),
            vmem((1, T), F32),
            vmem((NC, ROWS, HD), BF),
            vmem((NC, ROWS, HD), BF),
            vmem((NY, NZ, 16, T), BF),
            vmem((2, T, HD), F32),
            vmem((NC // GROUP, 3, T, GROUP * 16), BF),
            vmem((6, T, HD), F32),
            vmem((HL, T, HD), BF),
            vmem((HL, 2, T, HD), BF),
            vmem((2, HL, TXT, HD), BF),
            vmem((WINDOW, HL, 2, T, HD), BF),
            vmem((HL, T, HD), BF),
            vmem((HL, NH, T, HD), BF),
            vmem((HL, NH * HD, T), BF),
            dma((12,)),
            dma((2, NC)), dma((2, NC)),
            dma((NZ,)), dma((NZ,)), dma((NY,)), dma((NY,)),
            dma((NH,)), dma((NH,)), dma, dma,
            dma((WINDOW, HL)), dma((WINDOW, HL)), dma((HL,)), dma((HL,)),
            dma((HL, 4)), dma((HL, 4)), dma((HL, 4)), dma((HL, 4)),
        ],
        compiler_params=pltpu.CompilerParams(
            collective_id=0, has_side_effects=True, vmem_limit_bytes=56 << 20
        ),
        name="layer",
    )(
        qkv_tiles.transpose(1, 0, 2),
        seq_pos.reshape(1, T),
        rope_pos,
        text_keys,
        text_values,
        text_len,
        q_gain.reshape(1, HD),
        k_gain.reshape(1, HD),
        jnp.asarray(freq_row()),
        w_out.reshape(HL, HD, NH * T),
        b_out.reshape(1, T),
    )


def solution(mesh):
    in_specs = (
        P("ctx", None, "head"),
        P("ctx"),
        P(None, "ctx"),
        P("ctx", "head"),
        P("ctx", "head"),
        P(),
        P(),
        P(),
        P("head", None),
        P("head"),
    )
    return jax.shard_map(
        on_device, mesh=mesh, in_specs=in_specs, out_specs=P("ctx", "head"), check_vma=False
    )
```

```python
import functools

import jax
import jax.numpy as jnp
import numpy as np
from jax import lax
from jax.experimental import pallas as pl
from jax.experimental.pallas import tpu as pltpu
from jax.sharding import PartitionSpec as P

MESH = pl.DeviceIdType.MESH
BF = jnp.bfloat16
F32 = jnp.float32
NC = 32
NY, NZ = 4, 8
NH = 8
T = 384
HL = 3
HD = 128
CUT = 16
KV_ROWS = 160
ROWS = 224
WINDOW = 3
TXT = 256
TXD = 8
GROUP = 8
SCALE = float(np.log2(np.e) / np.sqrt(HD))

FAR = (4, 3, 5, 2, 6, 1, 7, 0)
OFFSETS = [(dy, dz) for dz in FAR for dy in (3, 2, 1, 0)]


def iota(shape, axis):
    return lax.broadcasted_iota(jnp.int32, shape, axis)


def onehot(mask):
    return jnp.where(mask, 1.0, 0.0).astype(BF)


def dot(a, b, ca=1, cb=0):
    return lax.dot_general(a, b, (((ca,), (cb,)), ((), ())), preferred_element_type=F32)


def partner_of(lane):
    up = (lane < 8) | ((lane >= 16) & (lane < 44)) | ((lane >= 72) & (lane < 100))
    half = jnp.where(lane < 16, 8, 28)
    return jnp.where(up, lane + half, lane - half), up


def partner_row(v):
    v = jnp.broadcast_to(v, (8, HD))
    lane = iota(v.shape, 1)
    _, up = partner_of(lane)
    near = jnp.where(up, pltpu.roll(v, HD - 8, 1), pltpu.roll(v, 8, 1))
    far = jnp.where(up, pltpu.roll(v, HD - 28, 1), pltpu.roll(v, 28, 1))
    return jnp.where(lane < 16, near, far)[0:1]


def rms_factor(x):
    return lax.rsqrt(jnp.mean(x * x, axis=-1, keepdims=True) + 1e-06)


def kernel(
    x_hbm, pos_hbm, rope_hbm, tk_hbm, tv_hbm, len_ref, qg_hbm, kg_hbm, freq_hbm, w_hbm, b_hbm,
    o_ref,
    x, pos_v, rope, rope_far, tk, tv, qg_v, kg_v, freq, bias,
    send, recv, tbuf, tab, puts, acc, qb, kv, text, win, stage, att, wv,
    isem, ssem, rsem, tzs, tzr, tys, tyr, wss, wrs, rs, rr,
    ws, wr, hs, hr, xs, xr, fs, fr,
):
    me = lax.axis_index("ctx")
    hd = lax.axis_index("head")
    my, mz = me // NZ, me % NZ
    core = hd % 2
    sib = hd + 1 - 2 * core

    def home(s):
        z = s % NZ
        return s - z + z + core * (NZ - 1 - 2 * z)

    mirror = my * NZ + NZ - 1 - mz
    shard_me = home(me)
    ahead = home((shard_me + 1) % NC)

    def at(offset):
        return ((my + offset[0]) % NY) * NZ + (mz + offset[1]) % NZ

    barrier = pltpu.get_barrier_semaphore()

    def greet_ctx(d, c):
        pl.semaphore_signal(barrier, inc=1, device_id=((me + d) % NC, hd), device_id_type=MESH)
        return c

    def greet_head(d, c):
        pl.semaphore_signal(barrier, inc=1, device_id=(me, (hd + d) % NH), device_id_type=MESH)
        return c

    fetch = [
        pltpu.make_async_copy(src, dst, isem.at[i])
        for i, (src, dst) in enumerate([
            (pos_hbm, pos_v), (x_hbm.at[1], x.at[1]), (kg_hbm, kg_v), (x_hbm.at[2], x.at[2]),
            (tk_hbm, tk), (tv_hbm, tv), (rope_hbm, rope), (x_hbm.at[0], x.at[0]),
            (freq_hbm, freq), (qg_hbm, qg_v), (b_hbm, bias),
            (
                w_hbm.at[:, :, pl.ds(pl.multiple_of(hd * T, T), T)],
                wv.at[:, pl.ds(pl.multiple_of(hd * HD, HD), HD), :],
            ),
        ])
    ]
    for copy in fetch:
        copy.start()
    lax.fori_loop(1, NC, greet_ctx, 0)
    lax.fori_loop(1, NH, greet_head, 0)

    fetch[0].wait()
    pos = pos_v[...].reshape(1, T)
    shard = ((pos >> 7) * 171) >> 9
    to_z = shard & (NZ - 1)
    dz = (to_z + core * (NZ - 1 - 2 * to_z) - mz) & (NZ - 1)
    dy = ((shard >> 3) - my) & (NY - 1)
    turn = jnp.zeros_like(dz)
    for place, far in enumerate(FAR):
        turn = jnp.where(dz == far, place, turn)
    index = turn * NY + NY - 1 - dy
    mine = iota((NC, T), 0) == index
    within = pos - shard * T
    first = jnp.min(jnp.where(mine, within, T), axis=1, keepdims=True)
    count = jnp.sum(jnp.where(mine, 1, 0), axis=1, keepdims=True)
    rank = within - jnp.sum(jnp.where(mine, first, 0), axis=0, keepdims=True)
    code_a = jnp.where(rank < CUT, index * 16 + rank, -1)
    code_b = jnp.where(rank < CUT, -1, index * 8 + rank - CUT)

    fetch[1].wait()
    fetch[2].wait()
    kg = kg_v[...]
    sub16 = iota((16, HD), 0)
    extra = jnp.zeros((16, HD), F32)
    for h in range(HL):
        k = x[1, :, h * HD:(h + 1) * HD].astype(F32)
        total = jnp.sum(k * rms_factor(k), axis=0, keepdims=True) * kg
        high = total.astype(BF).astype(F32)
        extra = jnp.where(sub16 == 9 + h, high, extra)
        extra = jnp.where(sub16 == 12 + h, total - high, extra)
    lane = iota((NC, HD), 1)
    meta = jnp.where(lane < 32, first >> 4, jnp.where(lane < 64, first & 15, count)).astype(F32)
    row3 = iota((GROUP, 16, HD), 1)

    def picks(g):
        a = onehot(iota((GROUP * 16, T), 0) + g * GROUP * 16 == code_a)
        return a, onehot(iota((GROUP * 8, T), 0) + g * GROUP * 8 == code_b)

    def early(part, c):
        return part[:, c * HD:(c + 1) * HD].astype(BF).reshape(GROUP, 16, HD)

    def late(part, c):
        return part[:, c * HD:(c + 1) * HD].reshape(GROUP, 8, HD)

    def both(a, b):
        return jnp.concatenate([a, b], axis=1).astype(BF)

    def pack_kv(g):
        pick_a, pick_b = picks(g)
        to = slice(g * GROUP, (g + 1) * GROUP)
        for comp in (1, 2):
            part = dot(pick_a, x[comp])
            for c in range(HL):
                base = ((comp - 1) * HL + c) * 16
                send[to, base:base + 16, :] = early(part, c)
        k, v = dot(pick_b, x[1]), dot(pick_b, x[2])
        send[to, 96:112, :] = both(late(k, 0), late(k, 1))
        send[to, 112:128, :] = both(late(k, 2), late(v, 0))
        send[to, 128:144, :] = both(late(v, 1), late(v, 2))
        q2 = late(dot(pick_b, x[0, :, 2 * HD:]), 0)
        info = jnp.where(row3 == 8, meta[to][:, None, :], extra[None])
        send[to, 144:160, :] = jnp.where(row3 < 8, jnp.concatenate([q2, q2], axis=1), info).astype(BF)

    def pack_q(g):
        pick_a, pick_b = picks(g)
        to = slice(g * GROUP, (g + 1) * GROUP)
        part = dot(pick_a, x[0])
        for c in range(HL):
            send[to, 160 + c * 16:176 + c * 16, :] = early(part, c)
        part = dot(pick_b, x[0, :, :2 * HD])
        send[to, 208:224, :] = both(late(part, 0), late(part, 1))

    fetch[3].wait()
    fetch[7].wait()
    pack_kv(0)
    fetch[4].wait()
    fetch[5].wait()
    tbuf[my, mz] = jnp.concatenate([tk[...].astype(F32), tv[...].astype(F32)], axis=0).astype(BF)
    fetch[6].wait()

    pl.semaphore_wait(barrier, NC - 1 + NH - 1)

    def text_z(d):
        z = (mz + d) % NZ
        return pltpu.make_async_remote_copy(
            src_ref=tbuf.at[my, mz], dst_ref=tbuf.at[my, mz], send_sem=tzs.at[d], recv_sem=tzr.at[d],
            device_id=(my * NZ + z, hd), device_id_type=MESH,
        )

    def text_y(d):
        y = (my + d) % NY
        return pltpu.make_async_remote_copy(
            src_ref=tbuf.at[my], dst_ref=tbuf.at[my], send_sem=tys.at[d], recv_sem=tyr.at[d],
            device_id=(y * NZ + mz, hd), device_id_type=MESH,
        )

    def piece(i, part):
        to = at(OFFSETS[i])
        rows = pl.ds(0, KV_ROWS) if part == 0 else pl.ds(KV_ROWS, ROWS - KV_ROWS)
        return pltpu.make_async_remote_copy(
            src_ref=send.at[i, rows], dst_ref=recv.at[i, rows],
            send_sem=ssem.at[part, i], recv_sem=rsem.at[part, i],
            device_id=(to, hd), device_id_type=MESH,
        )

    def weight(d):
        to = (hd + d) % NH
        return pltpu.make_async_remote_copy(
            src_ref=w_hbm.at[:, :, pl.ds(pl.multiple_of(to * T, T), T)],
            dst_ref=wv.at[:, pl.ds(pl.multiple_of(hd * HD, HD), HD), :],
            send_sem=wss.at[d], recv_sem=wrs.at[d],
            device_id=(me, to), device_id_type=MESH,
        )

    rope_swap = pltpu.make_async_remote_copy(
        src_ref=rope, dst_ref=rope_far, send_sem=rs, recv_sem=rr,
        device_id=(mirror, hd), device_id_type=MESH,
    )

    def shift(d, h):
        return pltpu.make_async_remote_copy(
            src_ref=kv.at[h] if d == 0 else win.at[d - 1, h], dst_ref=win.at[d, h],
            send_sem=ws.at[d, h], recv_sem=wr.at[d, h],
            device_id=(ahead, hd), device_id_type=MESH,
        )

    def go_home(h):
        return pltpu.make_async_remote_copy(
            src_ref=stage.at[h], dst_ref=att.at[h, hd], send_sem=hs.at[h], recv_sem=hr.at[h],
            device_id=(mirror, hd), device_id_type=MESH,
        )

    def spread(h, e):
        return pltpu.make_async_remote_copy(
            src_ref=att.at[h, hd], dst_ref=att.at[h, hd],
            send_sem=xs.at[h, e], recv_sem=xr.at[h, e],
            device_id=(me, (hd + 2 * e) % NH if e else sib), device_id_type=MESH,
        )

    def hand_on(h, e):
        g = (hd + NH - 2 * e) % NH
        return pltpu.make_async_remote_copy(
            src_ref=att.at[h, g], dst_ref=att.at[h, g],
            send_sem=fs.at[h, e], recv_sem=fr.at[h, e],
            device_id=(me, sib), device_id_type=MESH,
        )

    def each(make, n, act):
        def go(d, c):
            getattr(make(d), act)()
            return c
        lax.fori_loop(1, n, go, 0)

    def pieces(g):
        return range(g * GROUP, min((g + 1) * GROUP, NC - 1))

    GROUPS = NC // GROUP
    for i in pieces(0):
        piece(i, 0).start()
    rope_swap.start()
    each(text_z, NZ, "start")
    for g in range(1, GROUPS):
        pack_kv(g)
        for i in pieces(g):
            piece(i, 0).start()
    recv[NC - 1, 0:KV_ROWS] = send[NC - 1, 0:KV_ROWS]

    for g in range(GROUPS):
        pack_q(g)
        for i in pieces(g):
            piece(i, 1).start()
    recv[NC - 1, KV_ROWS:ROWS] = send[NC - 1, KV_ROWS:ROWS]
    each(weight, NH, "start")

    fetch[8].wait()
    fetch[9].wait()
    rope_swap.wait_recv()
    lane_t = iota((T, HD), 1)
    _, up = partner_of(lane_t)
    eye = iota((T, T), 0) == iota((T, T), 1)
    col = []
    for a in range(3):
        row = jnp.where(core == 1, rope_far[a:a + 1, :], rope[a:a + 1, :]).astype(F32)
        col.append(jnp.sum(jnp.where(eye, row, 0.0), axis=1, keepdims=True))
    angle = jnp.where(lane_t < 16, col[0], jnp.where(lane_t < 72, col[1], col[2])) * freq[...]
    tab[0] = jnp.cos(angle)
    sine = jnp.sin(angle)
    tab[1] = jnp.where(up, -sine, sine)
    li, lj = iota((HD, HD), 0), iota((HD, HD), 1)
    swap = onehot(li == partner_of(lj)[0])

    each(text_z, NZ, "wait_recv")
    each(text_y, NY, "start")

    W = GROUP * 16
    off = iota((1, W), 1) & 15
    offf = off.astype(F32)
    owner = (iota((GROUP, W), 1) >> 4) == iota((GROUP, W), 0)
    place = iota((T, W), 0).astype(F32)
    sums = jnp.zeros((16, HD), F32)

    def rows_of(g, base):
        return recv[g * GROUP:(g + 1) * GROUP, base:base + 16, :].reshape(W, HD)

    def put(g, blocks, high):
        rows = [jnp.concatenate([rows_of(g, a), rows_of(g, b)], axis=0) for a, b in blocks]
        where = jnp.concatenate([puts[g, 0], puts[g, 2 if high else 1]], axis=1)
        return dot(where, jnp.concatenate(rows, axis=1))

    for g in range(GROUPS):
        for i in pieces(g):
            piece(i, 0).wait_recv()
        tail = recv[g * GROUP:(g + 1) * GROUP, 144:160, :].astype(F32)
        sums = sums + jnp.sum(tail, axis=0)
        info = tail[:, 8, :]
        begin = jnp.sum(
            jnp.where(owner, info[:, 0:1] * 16.0 + info[:, 32:33], 0.0), axis=0, keepdims=True
        )
        size = jnp.sum(jnp.where(owner, info[:, 64:65], 0.0), axis=0, keepdims=True)
        puts[g, 0] = onehot(place == jnp.where(offf < size, begin + offf, -1.0))
        low = (off < 8) & (offf + 16.0 < size)
        puts[g, 1] = onehot(place == jnp.where(low, begin + offf + 16.0, -1.0))
        high = (off >= 8) & (offf + 8.0 < size)
        puts[g, 2] = onehot(place == jnp.where(high, begin + offf + 8.0, -1.0))
        for odd in range(2):
            part = put(g, [(c * 16, 96 + (c // 2) * 16) for c in (odd, odd + 2, odd + 4)], odd)
            acc[odd] = part if g == 0 else acc[odd] + part

    def block(c):
        return acc[c % 2, :, (c // 2) * HD:(c // 2 + 1) * HD]

    cos, sin = tab[0], tab[1]

    def rotated(rows, gain):
        pair = dot(rows.astype(BF), swap)
        return rms_factor(rows) * (rows * (cos * gain) + pair * (sin * partner_row(gain)))

    means = []
    for h in range(HL):
        mean = (sums[9 + h:10 + h] + sums[12 + h:13 + h]) * (1.0 / (NC * T))
        means.append(mean)
        k = rotated(block(h), kg) - (cos * mean + sin * partner_row(mean))
        kv[h, 0] = k.astype(BF)
        kv[h, 1] = block(3 + h).astype(BF)
        if h < 2:
            shift(0, h).start()

    each(text_y, NY, "wait_recv")
    for h in range(HL):
        both_t = tbuf[:, :, :, h * HD:(h + 1) * HD].astype(F32).reshape(NC, 16, HD)
        k = both_t[:, :TXD].reshape(TXT, HD)
        text[0, h] = (k * rms_factor(k) * kg - means[h]).astype(BF)
        v = jnp.where(iota((TXT, HD), 0) < len_ref[0], both_t[:, TXD:].reshape(TXT, HD), 0.0)
        text[1, h] = v.astype(BF)

    def forward(d, h):
        shift(d, h).wait_recv()
        if d < WINDOW - 1:
            shift(d + 1, h).start()

    forward(0, 0)
    forward(0, 1)
    shift(0, 2).start()

    qg = qg_v[...]
    rows = [None, None]
    for g in range(GROUPS):
        for i in pieces(g):
            piece(i, 1).wait_recv()
        for odd, blocks in enumerate((((160, 208), (192, 144)), ((176, 208),))):
            part = put(g, blocks, odd)
            rows[odd] = part if g == 0 else rows[odd] + part
    for h in range(HL):
        qb[h] = rotated(rows[h % 2][:, (h // 2) * HD:(h // 2 + 1) * HD], qg).astype(BF)

    ones = jnp.ones((T, HD), BF)
    live = onehot(iota((TXT, HD), 0) < len_ref[0])

    def weigh(h, k, v, beside):
        p = jnp.exp2(dot(qb[h], k, 1, 1) * SCALE)
        return dot(p.astype(BF), jnp.concatenate([v, beside], axis=1))

    num = {}
    for h in range(HL):
        num[h] = weigh(h, kv[h, 0], kv[h, 1], ones) + weigh(h, text[0, h], text[1, h], live)

    def attend(d, h):
        part = weigh(h, win[d, h, 0], win[d, h, 1], ones)
        num[h] = num[h] + jnp.where(shard_me > d, part, 0.0)

    def arrive(d, h):
        forward(d, h)
        attend(d, h)

    def spread_all(h):
        for e in (2, 1, 3, 0):
            spread(h, e).start()

    def finish(h):
        done = (num[h][:, :HD] / num[h][:, HD:]).astype(BF)

        @pl.when(core == 0)
        def _():
            att[h, hd] = done
            spread_all(h)

        @pl.when(core == 1)
        def _():
            stage[h] = done
            go_home(h).start()

    def relay(h):
        @pl.when(core == 1)
        def _():
            go_home(h).wait_recv()
            spread_all(h)

    def hand(h):
        for e in (1, 3, 2):
            spread(h, e).wait_recv()
            hand_on(h, e).start()

    def project(h):
        spread(h, 0).wait_recv()
        for e in (1, 3, 2):
            hand_on(h, e).wait_recv()
        rows = jnp.concatenate([att[h, g] for g in range(NH)], axis=1)
        return dot(rows, wv[h])

    attend(0, 0)
    attend(0, 1)
    arrive(1, 0)
    arrive(1, 1)
    arrive(0, 2)
    arrive(2, 0)
    finish(0)
    arrive(2, 1)
    finish(1)
    relay(0)
    for i in range(NC - 1):
        piece(i, 0).wait_send()
        piece(i, 1).wait_send()
    rope_swap.wait_send()
    each(text_z, NZ, "wait_send")
    each(text_y, NY, "wait_send")
    each(weight, NH, "wait_send")
    each(weight, NH, "wait_recv")
    fetch[10].wait()
    fetch[11].wait()
    arrive(1, 2)
    arrive(2, 2)
    finish(2)
    relay(1)
    hand(0)
    out = project(0) + bias[...].reshape(1, T)
    relay(2)
    hand(1)
    out = out + project(1)
    hand(2)
    out = out + project(2)
    o_ref[...] = out.astype(BF)

    for h in range(HL):
        for d in range(WINDOW):
            shift(d, h).wait_send()
        for e in range(4):
            spread(h, e).wait_send()
        for e in range(1, 4):
            hand_on(h, e).wait_send()

    @pl.when(core == 1)
    def _():
        for h in range(HL):
            go_home(h).wait_send()


def freq_row():
    row = np.zeros((1, HD), np.float32)
    offset = 0
    for width in (16, 56, 56):
        f = np.float32(256.0) ** (-np.arange(0, width, 2, dtype=np.float32) / np.float32(width))
        row[0, offset:offset + width] = np.concatenate([f, f])
        offset += width
    return row


def on_device(
    qkv_tiles, seq_pos, rope_pos, text_keys, text_values, text_len, q_gain, k_gain, w_out, b_out
):
    hbm = pl.BlockSpec(memory_space=pl.ANY)
    smem = pl.BlockSpec(memory_space=pltpu.SMEM)
    vmem = pltpu.VMEM
    dma = pltpu.SemaphoreType.DMA
    return pl.pallas_call(
        kernel,
        out_shape=jax.ShapeDtypeStruct((T, T), BF),
        in_specs=[hbm] * 5 + [smem] + [hbm] * 5,
        out_specs=pl.BlockSpec(memory_space=pltpu.VMEM),
        scratch_shapes=[
            vmem((3, T, T), BF),
            vmem((T,), jnp.int32),
            vmem((3, T), jnp.int32),
            vmem((3, T), jnp.int32),
            vmem((TXD, T), BF),
            vmem((TXD, T), BF),
            vmem((1, HD), F32),
            vmem((1, HD), F32),
            vmem((1, HD), F32),
            vmem((T,), F32),
            vmem((NC, ROWS, HD), BF),
            vmem((NC, ROWS, HD), BF),
            vmem((NY, NZ, 16, T), BF),
            vmem((2, T, HD), F32),
            vmem((NC // GROUP, 3, T, GROUP * 16), BF),
            vmem((2, T, T), F32),
            vmem((HL, T, HD), BF),
            vmem((HL, 2, T, HD), BF),
            vmem((2, HL, TXT, HD), BF),
            vmem((WINDOW, HL, 2, T, HD), BF),
            vmem((HL, T, HD), BF),
            vmem((HL, NH, T, HD), BF),
            vmem((HL, NH * HD, T), BF),
            dma((12,)),
            dma((2, NC)), dma((2, NC)),
            dma((NZ,)), dma((NZ,)), dma((NY,)), dma((NY,)),
            dma((NH,)), dma((NH,)), dma, dma,
            dma((WINDOW, HL)), dma((WINDOW, HL)), dma((HL,)), dma((HL,)),
            dma((HL, 4)), dma((HL, 4)), dma((HL, 4)), dma((HL, 4)),
        ],
        compiler_params=pltpu.CompilerParams(
            collective_id=0, has_side_effects=True, vmem_limit_bytes=56 << 20
        ),
        name="layer",
    )(
        qkv_tiles.transpose(1, 0, 2),
        seq_pos,
        rope_pos,
        text_keys,
        text_values,
        text_len,
        q_gain.reshape(1, HD),
        k_gain.reshape(1, HD),
        jnp.asarray(freq_row()),
        w_out.reshape(HL, HD, NH * T),
        b_out,
    )


def solution(mesh):
    in_specs = (
        P("ctx", None, "head"),
        P("ctx"),
        P(None, "ctx"),
        P("ctx", "head"),
        P("ctx", "head"),
        P(),
        P(),
        P(),
        P("head", None),
        P("head"),
    )
    return jax.shard_map(
        on_device, mesh=mesh, in_specs=in_specs, out_specs=P("ctx", "head"), check_vma=False
    )
```

```python
import functools

import jax
import jax.numpy as jnp
import numpy as np
from jax import lax
from jax.experimental import pallas as pl
from jax.experimental.pallas import tpu as pltpu
from jax.sharding import PartitionSpec as P

MESH = pl.DeviceIdType.MESH
BF = jnp.bfloat16
F32 = jnp.float32
NC = 32
NY, NZ = 4, 8
NH = 8
T = 384
HL = 3
HD = 128
CUT = 16
KV_ROWS = 160
ROWS = 224
WINDOW = 3
TXT = 256
TXD = 8
GROUP = 8
SCALE = float(np.log2(np.e) / np.sqrt(HD))

DY = (2, 1, 3, 0)
DZ = (3, 5, 4, 0, 1, 7, 2, 6)
OFFSETS = [(dy, dz) for dy in DY for dz in DZ]
OWN = OFFSETS.index((0, 0))

UNITS = ((0, 0, T), (1, 0, T), (2, 0, T // 2), (2, T // 2, T // 2))

STEPS = (
    "f00", "f01", "f02", "Q", "o0", "f10", "o1", "f11", "o2", "f12", "a00", "a01", "a02", "a10", "a11", "a12",
    "f20", "a20", "F0", "f21", "a21", "F1", "R0", "W", "f22", "a22", "F2", "a23", "F3", "R1", "H0", "R2",
    "R3", "H1", "H2", "H3", "P0", "P1", "P2", "P3",
)


def iota(shape, axis):
    return lax.broadcasted_iota(jnp.int32, shape, axis)


def onehot(mask):
    return jnp.where(mask, 1.0, 0.0).astype(BF)


def dot(a, b, ca=1, cb=0):
    return lax.dot_general(a, b, (((ca,), (cb,)), ((), ())), preferred_element_type=F32)


def partner_of(lane):
    up = (lane < 8) | ((lane >= 16) & (lane < 44)) | ((lane >= 72) & (lane < 100))
    half = jnp.where(lane < 16, 8, 28)
    return jnp.where(up, lane + half, lane - half), up


def partner_row(v):
    v = jnp.broadcast_to(v, (8, HD))
    lane = iota(v.shape, 1)
    _, up = partner_of(lane)
    near = jnp.where(up, pltpu.roll(v, HD - 8, 1), pltpu.roll(v, 8, 1))
    far = jnp.where(up, pltpu.roll(v, HD - 28, 1), pltpu.roll(v, 28, 1))
    return jnp.where(lane < 16, near, far)[0:1]


def rms_factor(x):
    return lax.rsqrt(jnp.mean(x * x, axis=-1, keepdims=True) + 1e-06)


def kernel(
    x_hbm, pos_hbm, rope_hbm, tk_hbm, tv_hbm, len_ref, qg_hbm, kg_hbm, freq_hbm, w_hbm, b_hbm,
    o_ref,
    x, pos_v, rope, rope_far, tk, tv, qg_v, kg_v, freq, bias,
    send, recv, tbuf, tab, puts, acc, qb, kv, text, win, stage, att, wv,
    isem, ssem, rsem, tzs, tzr, tys, tyr, wss, wrs, rs, rr,
    ws, wr, hs, hr, xs, xr, fs, fr,
):
    me = lax.axis_index("ctx")
    hd = lax.axis_index("head")
    my, mz = me // NZ, me % NZ
    core = hd % 2
    sib = hd + 1 - 2 * core

    def home(s):
        z = s % NZ
        return s - z + z + core * (NZ - 1 - 2 * z)

    mirror = my * NZ + NZ - 1 - mz
    shard_me = home(me)
    ahead = home((shard_me + 1) % NC)

    def at(offset):
        return ((my + offset[0]) % NY) * NZ + (mz + offset[1]) % NZ

    barrier = pltpu.get_barrier_semaphore()

    def greet_ctx(d, c):
        pl.semaphore_signal(barrier, inc=1, device_id=((me + d) % NC, hd), device_id_type=MESH)
        return c

    def greet_head(d, c):
        pl.semaphore_signal(barrier, inc=1, device_id=(me, (hd + d) % NH), device_id_type=MESH)
        return c

    fetch = [
        pltpu.make_async_copy(src, dst, isem.at[i])
        for i, (src, dst) in enumerate([
            (pos_hbm, pos_v), (x_hbm.at[1], x.at[1]), (kg_hbm, kg_v), (x_hbm.at[2], x.at[2]),
            (tk_hbm, tk), (tv_hbm, tv), (rope_hbm, rope), (x_hbm.at[0], x.at[0]),
            (freq_hbm, freq), (qg_hbm, qg_v), (b_hbm, bias),
            (
                w_hbm.at[:, :, pl.ds(pl.multiple_of(hd * T, T), T)],
                wv.at[:, pl.ds(pl.multiple_of(hd * HD, HD), HD), :],
            ),
        ])
    ]
    for copy in fetch:
        copy.start()
    lax.fori_loop(1, NC, greet_ctx, 0)
    lax.fori_loop(1, NH, greet_head, 0)

    fetch[0].wait()
    pos = pos_v[...].reshape(1, T)
    shard = ((pos >> 7) * 171) >> 9
    to_z = shard & (NZ - 1)
    dz = (to_z + core * (NZ - 1 - 2 * to_z) - mz) & (NZ - 1)
    dy = ((shard >> 3) - my) & (NY - 1)
    index = jnp.zeros_like(dz)
    for place, d in enumerate(DZ):
        index = jnp.where(dz == d, place, index)
    for place, d in enumerate(DY):
        index = jnp.where(dy == d, index + place * NZ, index)
    mine = iota((NC, T), 0) == index
    within = pos - shard * T
    first = jnp.min(jnp.where(mine, within, T), axis=1, keepdims=True)
    count = jnp.sum(jnp.where(mine, 1, 0), axis=1, keepdims=True)
    rank = within - jnp.sum(jnp.where(mine, first, 0), axis=0, keepdims=True)
    code_a = jnp.where(rank < CUT, index * 16 + rank, -1)
    code_b = jnp.where(rank < CUT, -1, index * 8 + rank - CUT)

    fetch[1].wait()
    fetch[2].wait()
    kg = kg_v[...]
    sub16 = iota((16, HD), 0)
    extra = jnp.zeros((16, HD), F32)
    for h in range(HL):
        k = x[1, :, h * HD:(h + 1) * HD].astype(F32)
        total = jnp.sum(k * rms_factor(k), axis=0, keepdims=True) * kg
        high = total.astype(BF).astype(F32)
        extra = jnp.where(sub16 == 9 + h, high, extra)
        extra = jnp.where(sub16 == 12 + h, total - high, extra)
    lane = iota((NC, HD), 1)
    meta = jnp.where(lane < 32, first >> 4, jnp.where(lane < 64, first & 15, count)).astype(F32)
    row3 = iota((GROUP, 16, HD), 1)

    def picks(g):
        a = onehot(iota((GROUP * 16, T), 0) + g * GROUP * 16 == code_a)
        return a, onehot(iota((GROUP * 8, T), 0) + g * GROUP * 8 == code_b)

    def early(part, c):
        return part[:, c * HD:(c + 1) * HD].astype(BF).reshape(GROUP, 16, HD)

    def late(part, c):
        return part[:, c * HD:(c + 1) * HD].reshape(GROUP, 8, HD)

    def both(a, b):
        return jnp.concatenate([a, b], axis=1).astype(BF)

    def pack_kv(g):
        pick_a, pick_b = picks(g)
        to = slice(g * GROUP, (g + 1) * GROUP)
        for comp in (1, 2):
            part = dot(pick_a, x[comp])
            for c in range(HL):
                base = ((comp - 1) * HL + c) * 16
                send[to, base:base + 16, :] = early(part, c)
        k, v = dot(pick_b, x[1]), dot(pick_b, x[2])
        send[to, 96:112, :] = both(late(k, 0), late(k, 1))
        send[to, 112:128, :] = both(late(k, 2), late(v, 0))
        send[to, 128:144, :] = both(late(v, 1), late(v, 2))
        q2 = late(dot(pick_b, x[0, :, 2 * HD:]), 0)
        info = jnp.where(row3 == 8, meta[to][:, None, :], extra[None])
        send[to, 144:160, :] = jnp.where(row3 < 8, jnp.concatenate([q2, q2], axis=1), info).astype(BF)

    def pack_q(g):
        pick_a, pick_b = picks(g)
        to = slice(g * GROUP, (g + 1) * GROUP)
        part = dot(pick_a, x[0])
        for c in range(HL):
            send[to, 160 + c * 16:176 + c * 16, :] = early(part, c)
        part = dot(pick_b, x[0, :, :2 * HD])
        send[to, 208:224, :] = both(late(part, 0), late(part, 1))

    fetch[3].wait()
    fetch[7].wait()
    pack_kv(0)
    fetch[4].wait()
    fetch[5].wait()
    tbuf[my, mz] = jnp.concatenate([tk[...].astype(F32), tv[...].astype(F32)], axis=0).astype(BF)
    fetch[6].wait()

    pl.semaphore_wait(barrier, NC - 1 + NH - 1)

    def text_z(d):
        z = (mz + d) % NZ
        return pltpu.make_async_remote_copy(
            src_ref=tbuf.at[my, mz], dst_ref=tbuf.at[my, mz], send_sem=tzs.at[d], recv_sem=tzr.at[d],
            device_id=(my * NZ + z, hd), device_id_type=MESH,
        )

    def text_y(d):
        y = (my + d) % NY
        return pltpu.make_async_remote_copy(
            src_ref=tbuf.at[my], dst_ref=tbuf.at[my], send_sem=tys.at[d], recv_sem=tyr.at[d],
            device_id=(y * NZ + mz, hd), device_id_type=MESH,
        )

    def piece(i, part):
        to = at(OFFSETS[i])
        rows = pl.ds(0, KV_ROWS) if part == 0 else pl.ds(KV_ROWS, ROWS - KV_ROWS)
        return pltpu.make_async_remote_copy(
            src_ref=send.at[i, rows], dst_ref=recv.at[i, rows],
            send_sem=ssem.at[part, i], recv_sem=rsem.at[part, i],
            device_id=(to, hd), device_id_type=MESH,
        )

    def weight(d):
        to = (hd + d) % NH
        return pltpu.make_async_remote_copy(
            src_ref=w_hbm.at[:, :, pl.ds(pl.multiple_of(to * T, T), T)],
            dst_ref=wv.at[:, pl.ds(pl.multiple_of(hd * HD, HD), HD), :],
            send_sem=wss.at[d], recv_sem=wrs.at[d],
            device_id=(me, to), device_id_type=MESH,
        )

    rope_swap = pltpu.make_async_remote_copy(
        src_ref=rope, dst_ref=rope_far, send_sem=rs, recv_sem=rr,
        device_id=(mirror, hd), device_id_type=MESH,
    )

    def shift(d, h):
        return pltpu.make_async_remote_copy(
            src_ref=kv.at[h] if d == 0 else win.at[d - 1, h], dst_ref=win.at[d, h],
            send_sem=ws.at[d, h], recv_sem=wr.at[d, h],
            device_id=(ahead, hd), device_id_type=MESH,
        )

    def slab(u, g):
        h, r, n = UNITS[u]
        return att.at[h, g, pl.ds(r, n)]

    def go_home(u):
        h, r, n = UNITS[u]
        return pltpu.make_async_remote_copy(
            src_ref=stage.at[h, pl.ds(r, n)], dst_ref=slab(u, hd), send_sem=hs.at[u], recv_sem=hr.at[u],
            device_id=(mirror, hd), device_id_type=MESH,
        )

    def spread(u, e):
        return pltpu.make_async_remote_copy(
            src_ref=slab(u, hd), dst_ref=slab(u, hd),
            send_sem=xs.at[u, e], recv_sem=xr.at[u, e],
            device_id=(me, (hd + 2 * e) % NH if e else sib), device_id_type=MESH,
        )

    def hand_on(u, e):
        g = (hd + NH - 2 * e) % NH
        return pltpu.make_async_remote_copy(
            src_ref=slab(u, g), dst_ref=slab(u, g),
            send_sem=fs.at[u, e], recv_sem=fr.at[u, e],
            device_id=(me, sib), device_id_type=MESH,
        )

    def each(make, n, act):
        def go(d, c):
            getattr(make(d), act)()
            return c
        lax.fori_loop(1, n, go, 0)

    def pieces(g):
        return [i for i in range(g * GROUP, (g + 1) * GROUP) if i != OWN]

    GROUPS = NC // GROUP
    for i in pieces(0):
        piece(i, 0).start()
    rope_swap.start()
    each(text_z, NZ, "start")
    for g in range(1, GROUPS):
        pack_kv(g)
        for i in pieces(g):
            piece(i, 0).start()
    recv[OWN, 0:KV_ROWS] = send[OWN, 0:KV_ROWS]

    for g in range(GROUPS):
        pack_q(g)
        for i in pieces(g):
            piece(i, 1).start()
    recv[OWN, KV_ROWS:ROWS] = send[OWN, KV_ROWS:ROWS]
    each(weight, NH, "start")

    fetch[8].wait()
    fetch[9].wait()
    rope_swap.wait_recv()
    lane_t = iota((T, HD), 1)
    _, up = partner_of(lane_t)
    eye = iota((T, T), 0) == iota((T, T), 1)
    col = []
    for a in range(3):
        row = jnp.where(core == 1, rope_far[a:a + 1, :], rope[a:a + 1, :]).astype(F32)
        col.append(jnp.sum(jnp.where(eye, row, 0.0), axis=1, keepdims=True))
    angle = jnp.where(lane_t < 16, col[0], jnp.where(lane_t < 72, col[1], col[2])) * freq[...]
    tab[0] = jnp.cos(angle)
    sine = jnp.sin(angle)
    tab[1] = jnp.where(up, -sine, sine)
    li, lj = iota((HD, HD), 0), iota((HD, HD), 1)
    swap = onehot(li == partner_of(lj)[0])

    each(text_z, NZ, "wait_recv")
    each(text_y, NY, "start")

    W = GROUP * 16
    off = iota((1, W), 1) & 15
    offf = off.astype(F32)
    owner = (iota((GROUP, W), 1) >> 4) == iota((GROUP, W), 0)
    place = iota((T, W), 0).astype(F32)
    sums = jnp.zeros((16, HD), F32)

    def rows_of(g, base):
        return recv[g * GROUP:(g + 1) * GROUP, base:base + 16, :].reshape(W, HD)

    def put(g, blocks, high):
        rows = [jnp.concatenate([rows_of(g, a), rows_of(g, b)], axis=0) for a, b in blocks]
        where = jnp.concatenate([puts[g, 0], puts[g, 2 if high else 1]], axis=1)
        return dot(where, jnp.concatenate(rows, axis=1))

    for g in range(GROUPS):
        for i in pieces(g):
            piece(i, 0).wait_recv()
        tail = recv[g * GROUP:(g + 1) * GROUP, 144:160, :].astype(F32)
        sums = sums + jnp.sum(tail, axis=0)
        info = tail[:, 8, :]
        begin = jnp.sum(
            jnp.where(owner, info[:, 0:1] * 16.0 + info[:, 32:33], 0.0), axis=0, keepdims=True
        )
        size = jnp.sum(jnp.where(owner, info[:, 64:65], 0.0), axis=0, keepdims=True)
        puts[g, 0] = onehot(place == jnp.where(offf < size, begin + offf, -1.0))
        low = (off < 8) & (offf + 16.0 < size)
        puts[g, 1] = onehot(place == jnp.where(low, begin + offf + 16.0, -1.0))
        high = (off >= 8) & (offf + 8.0 < size)
        puts[g, 2] = onehot(place == jnp.where(high, begin + offf + 8.0, -1.0))
        for odd in range(2):
            part = put(g, [(c * 16, 96 + (c // 2) * 16) for c in (odd, odd + 2, odd + 4)], odd)
            acc[odd] = part if g == 0 else acc[odd] + part

    def block(c):
        return acc[c % 2, :, (c // 2) * HD:(c // 2 + 1) * HD]

    cos, sin = tab[0], tab[1]

    def rotated(rows, gain):
        pair = dot(rows.astype(BF), swap)
        return rms_factor(rows) * (rows * (cos * gain) + pair * (sin * partner_row(gain)))

    means = []
    for h in range(HL):
        mean = (sums[9 + h:10 + h] + sums[12 + h:13 + h]) * (1.0 / (NC * T))
        means.append(mean)
        k = rotated(block(h), kg) - (cos * mean + sin * partner_row(mean))
        kv[h, 0] = k.astype(BF)
        kv[h, 1] = block(3 + h).astype(BF)
        shift(0, h).start()

    each(text_y, NY, "wait_recv")
    for h in range(HL):
        both_t = tbuf[:, :, :, h * HD:(h + 1) * HD].astype(F32).reshape(NC, 16, HD)
        k = both_t[:, :TXD].reshape(TXT, HD)
        text[0, h] = (k * rms_factor(k) * kg - means[h]).astype(BF)
        v = jnp.where(iota((TXT, HD), 0) < len_ref[0], both_t[:, TXD:].reshape(TXT, HD), 0.0)
        text[1, h] = v.astype(BF)

    def forward(d, h):
        shift(d, h).wait_recv()
        if d < WINDOW - 1:
            shift(d + 1, h).start()

    def queries():
        qg = qg_v[...]
        rows = [None, None]
        for g in range(GROUPS):
            for i in pieces(g):
                piece(i, 1).wait_recv()
            for odd, blocks in enumerate((((160, 208), (192, 144)), ((176, 208),))):
                part = put(g, blocks, odd)
                rows[odd] = part if g == 0 else rows[odd] + part
        for h in range(HL):
            qb[h] = rotated(rows[h % 2][:, (h // 2) * HD:(h // 2 + 1) * HD], qg).astype(BF)

    ones = jnp.ones((T, HD), BF)
    live = onehot(iota((TXT, HD), 0) < len_ref[0])

    def weigh(q, k, v, beside):
        p = jnp.exp2(dot(q, k, 1, 1) * SCALE)
        return dot(p.astype(BF), jnp.concatenate([v, beside], axis=1))

    num = {}

    def own(h):
        q = qb[h]
        num[h] = weigh(q, kv[h, 0], kv[h, 1], ones) + weigh(q, text[0, h], text[1, h], live)

    def attend(d, h, r=0, n=T):
        part = weigh(qb[h, r:r + n], win[d, h, 0], win[d, h, 1], ones)
        return num[h][r:r + n] + jnp.where(shard_me > d, part, 0.0)

    def finish(u, total):
        h, r, n = UNITS[u]
        done = (total[:, :HD] / total[:, HD:]).astype(BF)

        @pl.when(core == 0)
        def _():
            att[h, hd, r:r + n] = done
            spread_all(u)

        @pl.when(core == 1)
        def _():
            stage[h, r:r + n] = done
            go_home(u).start()

    def spread_all(u):
        for e in (2, 1, 3, 0):
            spread(u, e).start()

    def relay(u):
        @pl.when(core == 1)
        def _():
            go_home(u).wait_recv()
            spread_all(u)

    def hand(u):
        for e in (1, 3, 2):
            spread(u, e).wait_recv()
            hand_on(u, e).start()

    def project(u):
        h, r, n = UNITS[u]
        spread(u, 0).wait_recv()
        for e in (1, 3, 2):
            hand_on(u, e).wait_recv()
        rows = jnp.concatenate([att[h, g, r:r + n] for g in range(NH)], axis=1)
        return dot(rows, wv[h])

    def settle():
        for g in range(GROUPS):
            for i in pieces(g):
                piece(i, 0).wait_send()
                piece(i, 1).wait_send()
        rope_swap.wait_send()
        each(text_z, NZ, "wait_send")
        each(text_y, NY, "wait_send")
        each(weight, NH, "wait_send")
        each(weight, NH, "wait_recv")
        fetch[10].wait()
        fetch[11].wait()

    out = None
    last = {}
    for step in STEPS:
        kind, arg = step[0], [int(c) for c in step[1:]]
        if kind == "f":
            forward(*arg)
        elif kind == "Q":
            queries()
        elif kind == "o":
            own(*arg)
        elif kind == "a" and arg[0] < WINDOW - 1:
            num[arg[1]] = attend(*arg)
        elif kind == "a":
            last[arg[1]] = attend(arg[0], *UNITS[arg[1]])
        elif kind == "F":
            finish(arg[0], last[arg[0]])
        elif kind == "R":
            relay(*arg)
        elif kind == "W":
            settle()
        elif kind == "H":
            hand(*arg)
        elif kind == "P":
            h, r, n = UNITS[arg[0]]
            part = project(*arg)
            if h == 0:
                out = part + bias[...].reshape(1, T)
            elif h == 1:
                out = out + part
            else:
                o_ref[r:r + n] = (out[r:r + n] + part).astype(BF)

    for h in range(HL):
        for d in range(WINDOW):
            shift(d, h).wait_send()
    for u in range(len(UNITS)):
        for e in range(4):
            spread(u, e).wait_send()
        for e in range(1, 4):
            hand_on(u, e).wait_send()

    @pl.when(core == 1)
    def _():
        for u in range(len(UNITS)):
            go_home(u).wait_send()


def freq_row():
    row = np.zeros((1, HD), np.float32)
    offset = 0
    for width in (16, 56, 56):
        f = np.float32(256.0) ** (-np.arange(0, width, 2, dtype=np.float32) / np.float32(width))
        row[0, offset:offset + width] = np.concatenate([f, f])
        offset += width
    return row


def on_device(
    qkv_tiles, seq_pos, rope_pos, text_keys, text_values, text_len, q_gain, k_gain, w_out, b_out
):
    hbm = pl.BlockSpec(memory_space=pl.ANY)
    smem = pl.BlockSpec(memory_space=pltpu.SMEM)
    vmem = pltpu.VMEM
    dma = pltpu.SemaphoreType.DMA
    return pl.pallas_call(
        kernel,
        out_shape=jax.ShapeDtypeStruct((T, T), BF),
        in_specs=[hbm] * 5 + [smem] + [hbm] * 5,
        out_specs=pl.BlockSpec(memory_space=pltpu.VMEM),
        scratch_shapes=[
            vmem((3, T, T), BF),
            vmem((T,), jnp.int32),
            vmem((3, T), jnp.int32),
            vmem((3, T), jnp.int32),
            vmem((TXD, T), BF),
            vmem((TXD, T), BF),
            vmem((1, HD), F32),
            vmem((1, HD), F32),
            vmem((1, HD), F32),
            vmem((T,), F32),
            vmem((NC, ROWS, HD), BF),
            vmem((NC, ROWS, HD), BF),
            vmem((NY, NZ, 16, T), BF),
            vmem((2, T, HD), F32),
            vmem((NC // GROUP, 3, T, GROUP * 16), BF),
            vmem((2, T, T), F32),
            vmem((HL, T, HD), BF),
            vmem((HL, 2, T, HD), BF),
            vmem((2, HL, TXT, HD), BF),
            vmem((WINDOW, HL, 2, T, HD), BF),
            vmem((HL, T, HD), BF),
            vmem((HL, NH, T, HD), BF),
            vmem((HL, NH * HD, T), BF),
            dma((12,)),
            dma((2, NC)), dma((2, NC)),
            dma((NZ,)), dma((NZ,)), dma((NY,)), dma((NY,)),
            dma((NH,)), dma((NH,)), dma, dma,
            dma((WINDOW, HL)), dma((WINDOW, HL)), dma((4,)), dma((4,)),
            dma((4, 4)), dma((4, 4)), dma((4, 4)), dma((4, 4)),
        ],
        compiler_params=pltpu.CompilerParams(
            collective_id=0, has_side_effects=True, vmem_limit_bytes=56 << 20
        ),
        name="layer",
    )(
        qkv_tiles.transpose(1, 0, 2),
        seq_pos,
        rope_pos,
        text_keys,
        text_values,
        text_len,
        q_gain.reshape(1, HD),
        k_gain.reshape(1, HD),
        jnp.asarray(freq_row()),
        w_out.reshape(HL, HD, NH * T),
        b_out,
    )


def solution(mesh):
    in_specs = (
        P("ctx", None, "head"),
        P("ctx"),
        P(None, "ctx"),
        P("ctx", "head"),
        P("ctx", "head"),
        P(),
        P(),
        P(),
        P("head", None),
        P("head"),
    )
    return jax.shard_map(
        on_device, mesh=mesh, in_specs=in_specs, out_specs=P("ctx", "head"), check_vma=False
    )
```

```python
import functools

import jax
import jax.numpy as jnp
import numpy as np
from jax import lax
from jax.experimental import pallas as pl
from jax.experimental.pallas import tpu as pltpu
from jax.sharding import PartitionSpec as P

MESH = pl.DeviceIdType.MESH
BF = jnp.bfloat16
F32 = jnp.float32
NC = 32
NY, NZ = 4, 8
NH = 8
T = 384
HL = 3
HD = 128
CUT = 16
KV_ROWS = 160
ROWS = 224
WINDOW = 3
TXT = 256
TXD = 8
GROUP = 8
SCALE = float(np.log2(np.e) / np.sqrt(HD))

DY = (2, 1, 3, 0)
DZ = (3, 5, 4, 0, 1, 7, 2, 6)
OFFSETS = [(dy, dz) for dy in DY for dz in DZ]
OWN = OFFSETS.index((0, 0))

UNITS = ((0, 0, T), (1, 0, T), (2, 0, T // 2), (2, T // 2, T // 2))

STEPS = (
    "f00", "f01", "f02", "Q", "o0", "f10", "o1", "f11", "o2", "f12", "a00", "a01", "a02", "a10", "a11", "a12",
    "f20", "a20", "F0", "f21", "a21", "F1", "R0", "W", "f22", "a22", "F2", "a23", "F3", "R1", "H0", "R2",
    "R3", "H1", "Z", "H2", "H3", "P0", "P1", "P2", "P3",
)


def iota(shape, axis):
    return lax.broadcasted_iota(jnp.int32, shape, axis)


def onehot(mask):
    return jnp.where(mask, 1.0, 0.0).astype(BF)


def dot(a, b, ca=1, cb=0):
    return lax.dot_general(a, b, (((ca,), (cb,)), ((), ())), preferred_element_type=F32)


def partner_of(lane):
    up = (lane < 8) | ((lane >= 16) & (lane < 44)) | ((lane >= 72) & (lane < 100))
    half = jnp.where(lane < 16, 8, 28)
    return jnp.where(up, lane + half, lane - half), up


def partner_row(v):
    v = jnp.broadcast_to(v, (8, HD))
    lane = iota(v.shape, 1)
    _, up = partner_of(lane)
    near = jnp.where(up, pltpu.roll(v, HD - 8, 1), pltpu.roll(v, 8, 1))
    far = jnp.where(up, pltpu.roll(v, HD - 28, 1), pltpu.roll(v, 28, 1))
    return jnp.where(lane < 16, near, far)[0:1]


def rms_factor(x):
    return lax.rsqrt(jnp.mean(x * x, axis=-1, keepdims=True) + 1e-06)


def kernel(
    x_hbm, pos_hbm, rope_hbm, tk_hbm, tv_hbm, len_ref, qg_hbm, kg_hbm, freq_hbm, w_hbm, b_hbm,
    o_ref,
    x, pos_v, rope, rope_far, tk, tv, qg_v, kg_v, freq, bias,
    send, recv, tbuf, tab, puts, acc, qb, kv, text, win, stage, att, wv,
    isem, ssem, rsem, tzs, tzr, tys, tyr, wss, wrs, rs, rr,
    ws, wr, hs, hr, xs, xr, fs, fr,
):
    me = lax.axis_index("ctx")
    hd = lax.axis_index("head")
    my, mz = me // NZ, me % NZ
    core = hd % 2
    sib = hd + 1 - 2 * core

    def home(s):
        z = s % NZ
        return s - z + z + core * (NZ - 1 - 2 * z)

    mirror = my * NZ + NZ - 1 - mz
    shard_me = home(me)
    ahead = home((shard_me + 1) % NC)

    def at(offset):
        return ((my + offset[0]) % NY) * NZ + (mz + offset[1]) % NZ

    barrier = pltpu.get_barrier_semaphore()

    def greet_ctx(d, c):
        pl.semaphore_signal(barrier, inc=1, device_id=((me + d) % NC, hd), device_id_type=MESH)
        return c

    def greet_head(d, c):
        pl.semaphore_signal(barrier, inc=1, device_id=(me, (hd + d) % NH), device_id_type=MESH)
        return c

    fetch = [
        pltpu.make_async_copy(src, dst, isem.at[i])
        for i, (src, dst) in enumerate([
            (pos_hbm, pos_v), (x_hbm.at[1], x.at[1]), (kg_hbm, kg_v), (x_hbm.at[2], x.at[2]),
            (tk_hbm, tk), (tv_hbm, tv), (rope_hbm, rope), (x_hbm.at[0], x.at[0]),
            (freq_hbm, freq), (qg_hbm, qg_v), (b_hbm, bias),
            (
                w_hbm.at[:, :, pl.ds(pl.multiple_of(hd * T, T), T)],
                wv.at[:, pl.ds(pl.multiple_of(hd * HD, HD), HD), :],
            ),
        ])
    ]
    for copy in fetch:
        copy.start()
    lax.fori_loop(1, NC, greet_ctx, 0)
    lax.fori_loop(1, NH, greet_head, 0)

    fetch[0].wait()
    pos = pos_v[...].reshape(1, T)
    shard = ((pos >> 7) * 171) >> 9
    to_z = shard & (NZ - 1)
    dz = (to_z + core * (NZ - 1 - 2 * to_z) - mz) & (NZ - 1)
    dy = ((shard >> 3) - my) & (NY - 1)
    index = jnp.zeros_like(dz)
    for place, d in enumerate(DZ):
        index = jnp.where(dz == d, place, index)
    for place, d in enumerate(DY):
        index = jnp.where(dy == d, index + place * NZ, index)
    mine = iota((NC, T), 0) == index
    within = pos - shard * T
    first = jnp.min(jnp.where(mine, within, T), axis=1, keepdims=True)
    count = jnp.sum(jnp.where(mine, 1, 0), axis=1, keepdims=True)
    rank = within - jnp.sum(jnp.where(mine, first, 0), axis=0, keepdims=True)
    code_a = jnp.where(rank < CUT, index * 16 + rank, -1)
    code_b = jnp.where(rank < CUT, -1, index * 8 + rank - CUT)

    fetch[1].wait()
    fetch[2].wait()
    kg = kg_v[...]
    sub16 = iota((16, HD), 0)
    extra = jnp.zeros((16, HD), F32)
    for h in range(HL):
        k = x[1, :, h * HD:(h + 1) * HD].astype(F32)
        total = jnp.sum(k * rms_factor(k), axis=0, keepdims=True) * kg
        high = total.astype(BF).astype(F32)
        extra = jnp.where(sub16 == 9 + h, high, extra)
        extra = jnp.where(sub16 == 12 + h, total - high, extra)
    lane = iota((NC, HD), 1)
    meta = jnp.where(lane < 32, first >> 4, jnp.where(lane < 64, first & 15, count)).astype(F32)
    row3 = iota((GROUP, 16, HD), 1)

    def picks(g):
        a = onehot(iota((GROUP * 16, T), 0) + g * GROUP * 16 == code_a)
        return a, onehot(iota((GROUP * 8, T), 0) + g * GROUP * 8 == code_b)

    def early(part, c):
        return part[:, c * HD:(c + 1) * HD].astype(BF).reshape(GROUP, 16, HD)

    def late(part, c):
        return part[:, c * HD:(c + 1) * HD].reshape(GROUP, 8, HD)

    def both(a, b):
        return jnp.concatenate([a, b], axis=1).astype(BF)

    def pack_kv(g):
        pick_a, pick_b = picks(g)
        to = slice(g * GROUP, (g + 1) * GROUP)
        for comp in (1, 2):
            part = dot(pick_a, x[comp])
            for c in range(HL):
                base = ((comp - 1) * HL + c) * 16
                send[to, base:base + 16, :] = early(part, c)
        k, v = dot(pick_b, x[1]), dot(pick_b, x[2])
        send[to, 96:112, :] = both(late(k, 0), late(k, 1))
        send[to, 112:128, :] = both(late(k, 2), late(v, 0))
        send[to, 128:144, :] = both(late(v, 1), late(v, 2))
        q2 = late(dot(pick_b, x[0, :, 2 * HD:]), 0)
        info = jnp.where(row3 == 8, meta[to][:, None, :], extra[None])
        send[to, 144:160, :] = jnp.where(row3 < 8, jnp.concatenate([q2, q2], axis=1), info).astype(BF)

    def pack_q(g):
        pick_a, pick_b = picks(g)
        to = slice(g * GROUP, (g + 1) * GROUP)
        part = dot(pick_a, x[0])
        for c in range(HL):
            send[to, 160 + c * 16:176 + c * 16, :] = early(part, c)
        part = dot(pick_b, x[0, :, :2 * HD])
        send[to, 208:224, :] = both(late(part, 0), late(part, 1))

    fetch[3].wait()
    fetch[7].wait()
    pack_kv(0)
    fetch[4].wait()
    fetch[5].wait()
    tbuf[my, mz] = jnp.concatenate([tk[...].astype(F32), tv[...].astype(F32)], axis=0).astype(BF)
    fetch[6].wait()

    pl.semaphore_wait(barrier, NC - 1 + NH - 1)

    def text_z(d):
        z = (mz + d) % NZ
        return pltpu.make_async_remote_copy(
            src_ref=tbuf.at[my, mz], dst_ref=tbuf.at[my, mz], send_sem=tzs.at[d], recv_sem=tzr.at[d],
            device_id=(my * NZ + z, hd), device_id_type=MESH,
        )

    def text_y(d):
        y = (my + d) % NY
        return pltpu.make_async_remote_copy(
            src_ref=tbuf.at[my], dst_ref=tbuf.at[my], send_sem=tys.at[d], recv_sem=tyr.at[d],
            device_id=(y * NZ + mz, hd), device_id_type=MESH,
        )

    def piece(i, part):
        to = at(OFFSETS[i])
        rows = pl.ds(0, KV_ROWS) if part == 0 else pl.ds(KV_ROWS, ROWS - KV_ROWS)
        return pltpu.make_async_remote_copy(
            src_ref=send.at[i, rows], dst_ref=recv.at[i, rows],
            send_sem=ssem.at[part, i], recv_sem=rsem.at[part, i],
            device_id=(to, hd), device_id_type=MESH,
        )

    def weight(d):
        to = (hd + d) % NH
        return pltpu.make_async_remote_copy(
            src_ref=w_hbm.at[:, :, pl.ds(pl.multiple_of(to * T, T), T)],
            dst_ref=wv.at[:, pl.ds(pl.multiple_of(hd * HD, HD), HD), :],
            send_sem=wss.at[d], recv_sem=wrs.at[d],
            device_id=(me, to), device_id_type=MESH,
        )

    rope_swap = pltpu.make_async_remote_copy(
        src_ref=rope, dst_ref=rope_far, send_sem=rs, recv_sem=rr,
        device_id=(mirror, hd), device_id_type=MESH,
    )

    def shift(d, h):
        return pltpu.make_async_remote_copy(
            src_ref=kv.at[h] if d == 0 else win.at[d - 1, h], dst_ref=win.at[d, h],
            send_sem=ws.at[d, h], recv_sem=wr.at[d, h],
            device_id=(ahead, hd), device_id_type=MESH,
        )

    def slab(u, g):
        h, r, n = UNITS[u]
        return att.at[h, g, pl.ds(r, n)]

    def go_home(u):
        h, r, n = UNITS[u]
        return pltpu.make_async_remote_copy(
            src_ref=stage.at[h, pl.ds(r, n)], dst_ref=slab(u, hd), send_sem=hs.at[u], recv_sem=hr.at[u],
            device_id=(mirror, hd), device_id_type=MESH,
        )

    def spread(u, e):
        return pltpu.make_async_remote_copy(
            src_ref=slab(u, hd), dst_ref=slab(u, hd),
            send_sem=xs.at[u, e], recv_sem=xr.at[u, e],
            device_id=(me, (hd + 2 * e) % NH if e else sib), device_id_type=MESH,
        )

    def hand_on(u, e):
        g = (hd + NH - 2 * e) % NH
        return pltpu.make_async_remote_copy(
            src_ref=slab(u, g), dst_ref=slab(u, g),
            send_sem=fs.at[u, e], recv_sem=fr.at[u, e],
            device_id=(me, sib), device_id_type=MESH,
        )

    def each(make, n, act):
        def go(d, c):
            getattr(make(d), act)()
            return c
        lax.fori_loop(1, n, go, 0)

    def pieces(g):
        return [i for i in range(g * GROUP, (g + 1) * GROUP) if i != OWN]

    GROUPS = NC // GROUP
    for i in pieces(0):
        piece(i, 0).start()
    rope_swap.start()
    each(text_z, NZ, "start")
    for g in range(1, GROUPS):
        pack_kv(g)
        for i in pieces(g):
            piece(i, 0).start()
    recv[OWN, 0:KV_ROWS] = send[OWN, 0:KV_ROWS]

    for g in range(GROUPS):
        pack_q(g)
        for i in pieces(g):
            piece(i, 1).start()
    recv[OWN, KV_ROWS:ROWS] = send[OWN, KV_ROWS:ROWS]
    each(weight, NH, "start")

    fetch[8].wait()
    fetch[9].wait()
    rope_swap.wait_recv()
    lane_t = iota((T, HD), 1)
    _, up = partner_of(lane_t)
    eye = iota((T, T), 0) == iota((T, T), 1)
    col = []
    for a in range(3):
        row = jnp.where(core == 1, rope_far[a:a + 1, :], rope[a:a + 1, :]).astype(F32)
        col.append(jnp.sum(jnp.where(eye, row, 0.0), axis=1, keepdims=True))
    angle = jnp.where(lane_t < 16, col[0], jnp.where(lane_t < 72, col[1], col[2])) * freq[...]
    tab[0] = jnp.cos(angle)
    sine = jnp.sin(angle)
    tab[1] = jnp.where(up, -sine, sine)
    li, lj = iota((HD, HD), 0), iota((HD, HD), 1)
    swap = onehot(li == partner_of(lj)[0])

    each(text_z, NZ, "wait_recv")
    each(text_y, NY, "start")

    W = GROUP * 16
    off = iota((1, W), 1) & 15
    offf = off.astype(F32)
    owner = (iota((GROUP, W), 1) >> 4) == iota((GROUP, W), 0)
    place = iota((T, W), 0).astype(F32)
    sums = jnp.zeros((16, HD), F32)

    def rows_of(g, base):
        return recv[g * GROUP:(g + 1) * GROUP, base:base + 16, :].reshape(W, HD)

    def put(g, blocks, high):
        rows = [jnp.concatenate([rows_of(g, a), rows_of(g, b)], axis=0) for a, b in blocks]
        where = jnp.concatenate([puts[g, 0], puts[g, 2 if high else 1]], axis=1)
        return dot(where, jnp.concatenate(rows, axis=1))

    for g in range(GROUPS):
        for i in pieces(g):
            piece(i, 0).wait_recv()
        tail = recv[g * GROUP:(g + 1) * GROUP, 144:160, :].astype(F32)
        sums = sums + jnp.sum(tail, axis=0)
        info = tail[:, 8, :]
        begin = jnp.sum(
            jnp.where(owner, info[:, 0:1] * 16.0 + info[:, 32:33], 0.0), axis=0, keepdims=True
        )
        size = jnp.sum(jnp.where(owner, info[:, 64:65], 0.0), axis=0, keepdims=True)
        puts[g, 0] = onehot(place == jnp.where(offf < size, begin + offf, -1.0))
        low = (off < 8) & (offf + 16.0 < size)
        puts[g, 1] = onehot(place == jnp.where(low, begin + offf + 16.0, -1.0))
        high = (off >= 8) & (offf + 8.0 < size)
        puts[g, 2] = onehot(place == jnp.where(high, begin + offf + 8.0, -1.0))
        for odd in range(2):
            part = put(g, [(c * 16, 96 + (c // 2) * 16) for c in (odd, odd + 2, odd + 4)], odd)
            acc[odd] = part if g == 0 else acc[odd] + part

    def block(c):
        return acc[c % 2, :, (c // 2) * HD:(c // 2 + 1) * HD]

    cos, sin = tab[0], tab[1]

    def rotated(rows, gain):
        pair = dot(rows.astype(BF), swap)
        return rms_factor(rows) * (rows * (cos * gain) + pair * (sin * partner_row(gain)))

    means = []
    for h in range(HL):
        mean = (sums[9 + h:10 + h] + sums[12 + h:13 + h]) * (1.0 / (NC * T))
        means.append(mean)
        k = rotated(block(h), kg) - (cos * mean + sin * partner_row(mean))
        kv[h, 0] = k.astype(BF)
        kv[h, 1] = block(3 + h).astype(BF)
        shift(0, h).start()

    each(text_y, NY, "wait_recv")
    for h in range(HL):
        both_t = tbuf[:, :, :, h * HD:(h + 1) * HD].astype(F32).reshape(NC, 16, HD)
        k = both_t[:, :TXD].reshape(TXT, HD)
        text[0, h] = (k * rms_factor(k) * kg - means[h]).astype(BF)
        v = jnp.where(iota((TXT, HD), 0) < len_ref[0], both_t[:, TXD:].reshape(TXT, HD), 0.0)
        text[1, h] = v.astype(BF)

    def forward(d, h):
        shift(d, h).wait_recv()
        if d < WINDOW - 1:
            shift(d + 1, h).start()

    def queries():
        qg = qg_v[...]
        rows = [None, None]
        for g in range(GROUPS):
            for i in pieces(g):
                piece(i, 1).wait_recv()
            for odd, blocks in enumerate((((160, 208), (192, 144)), ((176, 208),))):
                part = put(g, blocks, odd)
                rows[odd] = part if g == 0 else rows[odd] + part
        for h in range(HL):
            qb[h] = rotated(rows[h % 2][:, (h // 2) * HD:(h // 2 + 1) * HD], qg).astype(BF)

    ones = jnp.ones((T, HD), BF)
    live = onehot(iota((TXT, HD), 0) < len_ref[0])

    def weigh(q, k, v, beside):
        p = jnp.exp2(dot(q, k, 1, 1) * SCALE)
        return dot(p.astype(BF), jnp.concatenate([v, beside], axis=1))

    num = {}

    def own(h):
        q = qb[h]
        num[h] = weigh(q, kv[h, 0], kv[h, 1], ones) + weigh(q, text[0, h], text[1, h], live)

    def attend(d, h, r=0, n=T):
        part = weigh(qb[h, r:r + n], win[d, h, 0], win[d, h, 1], ones)
        return num[h][r:r + n] + jnp.where(shard_me > d, part, 0.0)

    def finish(u, total):
        h, r, n = UNITS[u]
        done = (total[:, :HD] / total[:, HD:]).astype(BF)

        @pl.when(core == 0)
        def _():
            att[h, hd, r:r + n] = done
            spread_all(u)

        @pl.when(core == 1)
        def _():
            stage[h, r:r + n] = done
            go_home(u).start()

    def spread_all(u):
        for e in (2, 1, 3, 0):
            spread(u, e).start()

    def relay(u):
        @pl.when(core == 1)
        def _():
            go_home(u).wait_recv()
            spread_all(u)

    def hand(u):
        for e in (1, 3, 2):
            spread(u, e).wait_recv()
            hand_on(u, e).start()

    def project(u):
        h, r, n = UNITS[u]
        spread(u, 0).wait_recv()
        for e in (1, 3, 2):
            hand_on(u, e).wait_recv()
        rows = jnp.concatenate([att[h, g, r:r + n] for g in range(NH)], axis=1)
        return dot(rows, wv[h])

    def settle():
        for g in range(GROUPS):
            for i in pieces(g):
                piece(i, 0).wait_send()
                piece(i, 1).wait_send()
        rope_swap.wait_send()
        each(text_z, NZ, "wait_send")
        each(text_y, NY, "wait_send")
        each(weight, NH, "wait_send")
        each(weight, NH, "wait_recv")
        fetch[10].wait()
        fetch[11].wait()

    def left(u):
        for e in range(4):
            spread(u, e).wait_send()
        for e in range(1, 4):
            hand_on(u, e).wait_send()

        @pl.when(core == 1)
        def _():
            go_home(u).wait_send()

    out = None
    last = {}
    for step in STEPS:
        kind, arg = step[0], [int(c) for c in step[1:]]
        if kind == "f":
            forward(*arg)
        elif kind == "Z":
            for h in range(HL):
                for d in range(WINDOW):
                    shift(d, h).wait_send()
            left(0)
            left(1)
        elif kind == "Q":
            queries()
        elif kind == "o":
            own(*arg)
        elif kind == "a" and arg[0] < WINDOW - 1:
            num[arg[1]] = attend(*arg)
        elif kind == "a":
            last[arg[1]] = attend(arg[0], *UNITS[arg[1]])
        elif kind == "F":
            finish(arg[0], last[arg[0]])
        elif kind == "R":
            relay(*arg)
        elif kind == "W":
            settle()
        elif kind == "H":
            hand(*arg)
        elif kind == "P":
            h, r, n = UNITS[arg[0]]
            part = project(*arg)
            if h == 0:
                out = part + bias[...].reshape(1, T)
            elif h == 1:
                out = out + part
            else:
                o_ref[r:r + n] = (out[r:r + n] + part).astype(BF)

    left(2)
    left(3)


def freq_row():
    row = np.zeros((1, HD), np.float32)
    offset = 0
    for width in (16, 56, 56):
        f = np.float32(256.0) ** (-np.arange(0, width, 2, dtype=np.float32) / np.float32(width))
        row[0, offset:offset + width] = np.concatenate([f, f])
        offset += width
    return row


def on_device(
    qkv_tiles, seq_pos, rope_pos, text_keys, text_values, text_len, q_gain, k_gain, w_out, b_out
):
    hbm = pl.BlockSpec(memory_space=pl.ANY)
    smem = pl.BlockSpec(memory_space=pltpu.SMEM)
    vmem = pltpu.VMEM
    dma = pltpu.SemaphoreType.DMA
    return pl.pallas_call(
        kernel,
        out_shape=jax.ShapeDtypeStruct((T, T), BF),
        in_specs=[hbm] * 5 + [smem] + [hbm] * 5,
        out_specs=pl.BlockSpec(memory_space=pltpu.VMEM),
        scratch_shapes=[
            vmem((3, T, T), BF),
            vmem((T,), jnp.int32),
            vmem((3, T), jnp.int32),
            vmem((3, T), jnp.int32),
            vmem((TXD, T), BF),
            vmem((TXD, T), BF),
            vmem((1, HD), F32),
            vmem((1, HD), F32),
            vmem((1, HD), F32),
            vmem((T,), F32),
            vmem((NC, ROWS, HD), BF),
            vmem((NC, ROWS, HD), BF),
            vmem((NY, NZ, 16, T), BF),
            vmem((2, T, HD), F32),
            vmem((NC // GROUP, 3, T, GROUP * 16), BF),
            vmem((2, T, T), F32),
            vmem((HL, T, HD), BF),
            vmem((HL, 2, T, HD), BF),
            vmem((2, HL, TXT, HD), BF),
            vmem((WINDOW, HL, 2, T, HD), BF),
            vmem((HL, T, HD), BF),
            vmem((HL, NH, T, HD), BF),
            vmem((HL, NH * HD, T), BF),
            dma((12,)),
            dma((2, NC)), dma((2, NC)),
            dma((NZ,)), dma((NZ,)), dma((NY,)), dma((NY,)),
            dma((NH,)), dma((NH,)), dma, dma,
            dma((WINDOW, HL)), dma((WINDOW, HL)), dma((4,)), dma((4,)),
            dma((4, 4)), dma((4, 4)), dma((4, 4)), dma((4, 4)),
        ],
        compiler_params=pltpu.CompilerParams(
            collective_id=0, has_side_effects=True, vmem_limit_bytes=56 << 20
        ),
        name="layer",
    )(
        qkv_tiles.transpose(1, 0, 2),
        seq_pos,
        rope_pos,
        text_keys,
        text_values,
        text_len,
        q_gain.reshape(1, HD),
        k_gain.reshape(1, HD),
        jnp.asarray(freq_row()),
        w_out.reshape(HL, HD, NH * T),
        b_out,
    )


def solution(mesh):
    in_specs = (
        P("ctx", None, "head"),
        P("ctx"),
        P(None, "ctx"),
        P("ctx", "head"),
        P("ctx", "head"),
        P(),
        P(),
        P(),
        P("head", None),
        P("head"),
    )
    return jax.shard_map(
        on_device, mesh=mesh, in_specs=in_specs, out_specs=P("ctx", "head"), check_vma=False
    )
```
